1024 devices in a mesh: dp: 8 (over z), pipe: 16 (over y, core), expert: 8 (over x).
Axes of the slice: x: 8, y: 8, z: 8, core: 2. Of those that a mesh axis runs over, the one named last changes fastest.
Arguments:
- tokens: bfloat16 [6144, 3072], P(('dp', 'expert')), may hold values from -6 to 6
- routes: int32 [6144, 2], P(('dp', 'expert')), may hold values from 0 to 7, all different within a row; in each aligned block of 96 rows (0 to 95, 96 to 191, ...) at most 32 rows name the same one
- route_weights: float32 [6144, 2], P(('dp', 'expert')), may hold values from 0.2 to 1
- w_gate: bfloat16 [8, 3072, 8192], P('expert', None, 'pipe'), may hold values from -0.109375 to 0.109375
- w_up: bfloat16 [8, 3072, 8192], P('expert', None, 'pipe'), may hold values from -0.109375 to 0.109375
- w_down: bfloat16 [8, 8192, 3072], P('expert', 'pipe'), may hold values from -0.0625 to 0.0625
Outputs:
- mixed: bfloat16 [6144, 3072], P(('dp', 'expert'), 'pipe')
The draws below stay inside these ranges and needn't reach their ends.
Inputs may be any that keep to these rules, and one draw needn't show every extreme that they name: `routes`: each row names two different experts. Among the 96 rows of one block no expert is named more than 32 times, a bound that some block reaches.
All inputs are finite; a program needn't handle non-finite values.
Results may differ from the reference program's by a relative error of at most 0.019.
Values may be sent and summed in bfloat16 or wider, within the bound.
A program may use at most 64 MiB of HBM per device.

```python
import math
import jax
import jax.numpy as jnp
import numpy as np
from jax import lax

D = 3072
FF = 8192
TOK_DEV = 96
EXPERTS = 8
CAP = 32
FF_DEV = 512
TOKENS = 6144


def shard_levels(stream_key, shape, pieces, low, largest):
    def one(axis_at, parts):
        heights = jax.random.uniform(jax.random.fold_in(jax.random.fold_in(stream_key, 6), axis_at), (parts,), jnp.float32, low / len(pieces), largest / len(pieces))
        return jnp.repeat(jnp.exp(heights), shape[axis_at] // parts).reshape((-1,) + (1,) * (len(shape) - axis_at - 1))

    loudness = one(*pieces[0])
    for cut in pieces[1:]:
        loudness = loudness * one(*cut)
    return loudness


def deal_out(stream_key, own, number, rows, count, top, reach, skew):
    order = jax.random.permutation(stream_key, count)
    crowded, ordinary = load_shares(count, rows * top, reach, skew, True), load_shares(count, rows * top, reach, skew, False)
    places = jnp.arange(count)

    def named(tallies, offset_by):
        used = int((tallies > 0).sum())
        fixed = max(1, used // 4)
        moved = fixed + (places - fixed + offset_by * (used - fixed)) % max(1, count - fixed)
        return jnp.zeros((count,), jnp.int32).at[order[jnp.where(places < fixed, places, moved)]].set(jnp.asarray(tallies, jnp.int32))

    tallies = jnp.where(number % 4 == 0, named(crowded, number // 4), named(ordinary, number - number // 4 - 1))
    mixed = jax.random.permutation(jax.random.fold_in(own, 3), count)
    source_of, receiver = mixed[0:count // 2 * 2:2], mixed[1:count // 2 * 2:2]
    margin = jnp.minimum(tallies[source_of] - 1, reach - tallies[receiver]) // 2
    margin = jnp.where((source_of == order[0]) | (receiver == order[0]) | (tallies[receiver] == 0), 0, jnp.maximum(margin, 0))
    moved = jax.random.randint(jax.random.fold_in(own, 4), (count // 2,), 0, 1 << 20) % (margin + 1)
    tallies = tallies.at[source_of].add(-moved).at[receiver].add(moved)
    labels = jnp.searchsorted(jnp.cumsum(tallies), jnp.arange(rows * top), side="right").astype(jnp.int32)
    table = labels.reshape(top, rows).T
    table = table[jax.random.permutation(jax.random.fold_in(own, 1), rows)]
    offset_by = jax.random.randint(jax.random.fold_in(own, 2), (rows, 1), 0, top)
    return jnp.take_along_axis(table, (jnp.arange(top)[None, :] + offset_by) % top, axis=1)


def load_shares(number_of, total, most, lean, full):
    portions = [(1 << 20) // math.isqrt(grade ** lean) + 1 for grade in range(1, number_of + 1)]
    largest = most if full else min(most, max(-(-total // number_of), total * portions[0] // sum(portions)))
    least = 1 if total - largest >= number_of - 1 else 0
    counts, spare = [largest] + [least] * (number_of - 1), total - largest - least * (number_of - 1)
    while spare > 0:
        movable = [i for i in range(1, number_of) if counts[i] < largest] or [i for i in range(1, number_of) if counts[i] < most]
        whole, left = sum([portions[i] for i in movable]), spare
        for i in movable:
            more = min(most - counts[i], max(1, left * portions[i] // whole), spare)
            counts[i] = counts[i] + more
            spare = spare - more
    return np.array(counts)


def normal_values(own_key, dims, scale, reach, shards=(), kind=jnp.bfloat16):
    drawn = jax.random.normal(own_key, dims, jnp.float32) * scale
    if len(shards) > 0:
        drawn = shard_levels(own_key, dims, shards, -0.22, 0.18) * drawn
    return jnp.clip(drawn, min=-reach, max=reach).astype(kind)


def setup_inputs(seed: int = 0) -> dict:
    key_of = jax.random.split(jax.random.key(seed), 7)
    tokens = normal_values(key_of[0], (TOKENS, D), 1.0, 6.0, ((0, 64),))
    routes_keys = jax.random.split(jax.random.fold_in(key_of[1], 1), TOKENS // TOK_DEV)
    routes_turns = jax.random.permutation(jax.random.fold_in(key_of[1], 3), TOKENS // TOK_DEV)
    routes = jax.vmap(lambda own, number: deal_out(jax.random.fold_in(key_of[1], 2), own, number, TOK_DEV, EXPERTS, 2, CAP, 1))(routes_keys, routes_turns).reshape((TOKENS, 2))
    route_weights = jnp.clip(0.2 + 0.8 * jax.random.uniform(key_of[2], (TOKENS, 2), jnp.float32) ** shard_levels(key_of[2], (TOKENS, 2), ((0, 64),), -0.2, 0.2), 0.2, 1.0)
    w_gate = normal_values(key_of[3], (EXPERTS, D, FF), D ** -0.5, 0.109375, ((0, 8), (2, 16)))
    w_up = normal_values(key_of[4], (EXPERTS, D, FF), D ** -0.5, 0.109375, ((0, 8), (2, 16)))
    w_down = normal_values(key_of[5], (EXPERTS, FF, D), FF ** -0.5, 0.0625, ((0, 8), (1, 16)))
    return {"tokens": tokens, "routes": routes, "route_weights": route_weights, "w_gate": w_gate, "w_up": w_up, "w_down": w_down}


def reference(tokens, routes, route_weights, w_gate, w_up, w_down):
    blocks = TOKENS // TOK_DEV
    choices = routes.reshape(blocks, TOK_DEV * 2).astype(jnp.int32)
    expert_ids = jnp.arange(EXPERTS, dtype=jnp.int32)
    matches = (choices[:, None, :] == expert_ids[None, :, None]).astype(jnp.int32)
    rank_of = (jnp.cumsum(matches, axis=2) - 1).astype(jnp.int32)
    slot_of = jnp.sum(rank_of * matches, axis=1).astype(jnp.int32)
    doubled = jnp.repeat(tokens.reshape(blocks, TOK_DEV, D), 2, axis=1).astype(jnp.float32)
    slot_ids = jnp.arange(CAP, dtype=jnp.int32)
    hidden_blocks = FF // FF_DEV

    def one_expert(packed):
        expert_index, gate_w, up_w, down_w = packed
        picker = ((choices == expert_index)[:, None, :] & (slot_of[:, None, :] == slot_ids[None, :, None])).astype(jnp.float32)
        buffer_rows = jnp.einsum("sca,sad->scd", picker, doubled).astype(jnp.bfloat16).reshape(blocks * CAP, D)
        gate_values = jnp.dot(buffer_rows, gate_w, preferred_element_type=jnp.float32)
        up_values = jnp.dot(buffer_rows, up_w, preferred_element_type=jnp.float32)
        hidden = (jax.nn.silu(gate_values) * up_values).astype(jnp.bfloat16)
        hidden_split = hidden.reshape(blocks * CAP, hidden_blocks, FF_DEV).transpose(1, 0, 2)
        down_split = down_w.reshape(hidden_blocks, FF_DEV, D)

        def add_block(running, paired):
            hidden_piece, down_piece = paired
            block_term = jnp.dot(hidden_piece, down_piece, preferred_element_type=jnp.float32).astype(jnp.bfloat16)
            block_term = lax.optimization_barrier(block_term)
            return running + block_term.astype(jnp.float32), None

        running, _ = lax.scan(add_block, jnp.zeros((blocks * CAP, D), jnp.float32), (hidden_split, down_split))
        return running.astype(jnp.bfloat16).reshape(blocks, CAP, D)

    expert_out = lax.map(one_expert, (expert_ids, w_gate, w_up, w_down))
    block_ids = (jnp.arange(TOKENS, dtype=jnp.int32) // TOK_DEV).astype(jnp.int32)
    slot_pairs = slot_of.reshape(TOKENS, 2)
    first_out = expert_out[routes[:, 0], block_ids, slot_pairs[:, 0]].astype(jnp.float32)
    second_out = expert_out[routes[:, 1], block_ids, slot_pairs[:, 1]].astype(jnp.float32)
    mixed = route_weights[:, 0:1] * first_out + route_weights[:, 1:2] * second_out
    return mixed.astype(jnp.bfloat16)
```

```python
import functools

import jax
import jax.numpy as jnp
from jax import lax
from jax.experimental import pallas as pl
from jax.experimental.pallas import tpu as pltpu
from jax.sharding import PartitionSpec as P

MESH = pl.DeviceIdType.MESH
F32 = jnp.float32
BF16 = jnp.bfloat16


def kernel(
    dims,
    tokens,
    routes,
    route_w,
    wg,
    wu,
    wd,
    out,
    tok_v,
    xs,
    xbuf,
    wg_v,
    wu_v,
    wd_v,
    acc_g,
    acc_u,
    hid,
    mix,
    pk,
    cin,
    rin,
    rout,
    fin,
    rbuf,
    load_sem,
    xs_sem,
    xr_sem,
    os_sem,
    or_sem,
    ys_sem,
    yr_sem,
    cs_sem,
    cr_sem,
    ds_sem,
    dr_sem,
    rs_sem,
    rr_sem,
    fs_sem,
    fr_sem,
):
    ne, ny, half, width = dims
    rows = ne * half
    sub = rows // 2
    pipe = lax.axis_index("pipe")
    e = lax.axis_index("expert")
    y = pipe // 2
    c = pipe % 2
    right = {"pipe": (y + 1) % ny * 2 + c}
    left = {"pipe": (y + ny - 1) % ny * 2 + c}
    peer = {"pipe": 2 * y + 1 - c}
    far = ny // 2
    hop = far - 1

    def chunk(j):
        return (y + j + ny) % ny

    def at16(x):
        return pl.multiple_of(x, 16)

    def remote(src, dst, send, recv, device):
        return pltpu.make_async_remote_copy(
            src_ref=src, dst_ref=dst, send_sem=send, recv_sem=recv, device_id=device, device_id_type=MESH
        )

    sent = []

    def go(copy):
        copy.start()
        sent.append(copy)

    barrier = pltpu.get_barrier_semaphore()
    for device in [{"expert": (e + j) % ne} for j in range(1, ne)] + [right, left, peer]:
        pl.semaphore_signal(barrier, inc=1, device_id=device, device_id_type=MESH)

    loads = []
    for i, j in enumerate((0, far)):
        cols = pl.ds(pl.multiple_of(chunk(j) * width, 128), width)
        loads.append(pltpu.make_async_copy(tokens.at[:, cols], tok_v.at[i], load_sem.at[i]))
    for i, (src, dst) in enumerate(((wg, wg_v), (wu, wu_v), (wd, wd_v))):
        loads.append(pltpu.make_async_copy(src.at[0], dst, load_sem.at[2 + i]))
    for copy in loads:
        copy.start()

    toks = routes.shape[0]
    lane = lax.broadcasted_iota(jnp.int32, (toks, 2 * rows), 1)
    hbits, rbits = half.bit_length() - 1, rows.bit_length() - 1
    expert_of = (lane >> hbits) & (ne - 1)
    slot_of = ((lane >> rbits) << hbits) + (lane & (half - 1))
    first = routes[:, 0:1] == expert_of
    second = routes[:, 1:2] == expert_of
    named = jnp.logical_or(first, second)
    before = (
        lax.broadcasted_iota(jnp.int32, (toks, toks), 0) > lax.broadcasted_iota(jnp.int32, (toks, toks), 1)
    ).astype(F32)
    rank = jnp.dot(before.astype(BF16), named.astype(F32).astype(BF16), preferred_element_type=F32)
    taken = jnp.logical_and(named, rank == slot_of.astype(F32))
    mix[...] = jnp.where(taken, jnp.where(first, route_w[:, 0:1], route_w[:, 1:2]), 0.0)
    picked = taken.astype(F32)
    mine = jnp.where(c == 0, picked[:, :rows], picked[:, rows:]).astype(BF16)
    for i in range(2):
        loads[i].wait()
        xs[i] = lax.dot_general(
            mine, tok_v[i], (((0,), (0,)), ((), ())), preferred_element_type=F32
        ).astype(BF16)

    pl.semaphore_wait(barrier, ne - 1 + 3)

    own_rows = pl.ds(at16(c * rows + e * half), half)
    for i, j, send, recv in ((0, 0, xs_sem, xr_sem), (1, far, os_sem, or_sem)):
        for n in range(1, ne):
            t = (e + n) % ne
            go(
                remote(
                    xs.at[i, pl.ds(at16(t * half), half)],
                    xbuf.at[chunk(j), own_rows],
                    send.at[n],
                    recv.at[n],
                    {"expert": t},
                )
            )
        xbuf[chunk(j), own_rows, :] = xs[i, pl.ds(at16(e * half), half), :]

    def x_arrived(i, j, send, recv):
        for n in range(1, ne):
            s = (e + ne - n) % ne
            where = pl.ds(at16(c * rows + s * half), half)
            remote(xs.at[i, pl.ds(0, half)], xbuf.at[chunk(j), where], send.at[n], recv.at[n], {"expert": s}).wait_recv()

    def piece(b):
        return pl.ds(at16(c * rows + b * sub), sub)

    def y_copy(way, s, b):
        j = -s if way == 0 else s
        ref = xbuf.at[chunk(j), piece(b)]
        return remote(ref, ref, ys_sem.at[way, s, b], yr_sem.at[way, s, b], right if way == 0 else left)

    def y_arrived(way, s, b):
        j = -1 - s if way == 0 else s + 1
        ref = xbuf.at[chunk(j), piece(b)]
        remote(ref, ref, ys_sem.at[way, s, b], yr_sem.at[way, s, b], right if way == 0 else left).wait_recv()

    def share(j):
        ref = xbuf.at[chunk(j), pl.ds(at16(c * rows), rows)]
        return remote(ref, ref, cs_sem.at[j + hop], cr_sem.at[j + hop], peer)

    def shared(j):
        ref = xbuf.at[chunk(j), pl.ds(at16((1 - c) * rows), rows)]
        remote(ref, ref, cs_sem.at[j + hop], cr_sem.at[j + hop], peer).wait_recv()

    def gemm(j, start=False):
        k = chunk(j)
        shared(j)
        lhs = xbuf[k]
        deep = pl.ds(pl.multiple_of(k * width, 128), width)
        for acc, w in ((acc_g, wg_v), (acc_u, wu_v)):
            term = jnp.dot(lhs, w[deep, :], preferred_element_type=F32)
            acc[...] = term if start else acc[...] + term

    x_arrived(0, 0, xs_sem, xr_sem)
    for b in range(2):
        for way in range(2):
            go(y_copy(way, 0, b))
    go(share(0))
    loads[2].wait()
    loads[3].wait()
    gemm(0, True)
    for s in range(hop):
        for b in range(2):
            for way in range(2):
                y_arrived(way, s, b)
                if s + 1 < hop:
                    go(y_copy(way, s + 1, b))
        go(share(-1 - s))
        go(share(s + 1))
        if s == 0:
            x_arrived(1, far, os_sem, or_sem)
            go(share(far))
            gemm(far)
        gemm(-1 - s)
        gemm(s + 1)

    gate = acc_g[...]
    hid[...] = (gate / (1.0 + jnp.exp(-gate)) * acc_u[...]).astype(BF16)
    loads[4].wait()

    low = lax.broadcasted_iota(jnp.int32, (rows, width), 1) < width // 2

    def down(j):
        i = j + hop
        cols = pl.ds(pl.multiple_of(chunk(j) * width, 128), width)
        part = jnp.dot(hid[...], wd_v[:, cols], preferred_element_type=F32)
        a, b = part[:rows], part[rows:]
        pk[i, 0] = jnp.where(low, a, pltpu.roll(b, width // 2, 1)).astype(BF16)
        pk[i, 1] = jnp.where(low, pltpu.roll(a, width // 2, 1), b).astype(BF16)
        go(remote(pk.at[i, 1 - c], cin.at[i], ds_sem.at[i], dr_sem.at[i], peer))

    def met(j):
        i = j + hop
        remote(pk.at[i, 1 - c], cin.at[i], ds_sem.at[i], dr_sem.at[i], peer).wait_recv()

    def own(j, b):
        i = j + hop
        at = pl.ds(b * sub, sub)
        return pk[i, c, at, :].astype(F32) + cin[i, at, :].astype(F32)

    def r_copy(way, s, b):
        at = pl.ds(b * sub, sub)
        return remote(
            rout.at[way, s, at],
            rin.at[way, s, at],
            rs_sem.at[way, s, b],
            rr_sem.at[way, s, b],
            right if way == 0 else left,
        )

    def got(way, s, b):
        r_copy(way, s, b).wait_recv()
        return rin[way, s, pl.ds(b * sub, sub), :].astype(F32)

    def pass_on(way, s, b):
        if s == 0:
            total = own(far, b)
        else:
            total = own(far - s if way == 0 else s - far, b)
            if s > 1 or b == way:
                total = total + got(way, s - 1, b)
        rout[way, s, pl.ds(b * sub, sub), :] = total.astype(BF16)
        go(r_copy(way, s, b))

    down(far)
    down(far - 1)
    down(1 - far)
    met(far)
    pass_on(0, 0, 0)
    pass_on(1, 0, 1)
    met(far - 1)
    pass_on(0, 1, 1)
    met(1 - far)
    pass_on(1, 1, 0)
    for j in range(far - 2, 0, -1):
        down(j)
        down(-j)
    down(0)
    pass_on(0, 1, 0)
    pass_on(1, 1, 1)
    for s in range(2, far):
        met(far - s)
        met(s - far)
        for b in (1, 0):
            pass_on(0, s, b)
            pass_on(1, s, 1 - b)
    met(0)
    for b in range(2):
        total = own(0, b) + got(0, far - 1, b) + got(1, far - 1, b)
        fin[pl.ds(b * sub, sub), :] = total.astype(BF16)

    for n in range(1, ne):
        t = (e + n) % ne
        go(
            remote(
                fin.at[pl.ds(at16(t * half), half)],
                rbuf.at[pl.ds(at16(e * half), half)],
                fs_sem.at[n],
                fr_sem.at[n],
                {"expert": t},
            )
        )
    rbuf[pl.ds(at16(e * half), half), :] = fin[pl.ds(at16(e * half), half), :]
    hi = mix[...].astype(BF16)
    lo = (mix[...] - hi.astype(F32)).astype(BF16)
    for n in range(1, ne):
        s = (e + ne - n) % ne
        remote(
            fin.at[pl.ds(0, half)], rbuf.at[pl.ds(at16(s * half), half)], fs_sem.at[n], fr_sem.at[n], {"expert": s}
        ).wait_recv()
    back = rbuf[...]

    def mixed(side):
        cols = slice(side * rows, side * rows + rows)
        return jnp.dot(hi[:, cols], back, preferred_element_type=F32) + jnp.dot(
            lo[:, cols], back, preferred_element_type=F32
        )

    total = mixed(0) + pltpu.roll(mixed(1), width // 2, 1)
    out[...] = total[:, : width // 2].astype(BF16)
    for copy in sent:
        copy.wait_send()


def on_device(tokens, routes, route_weights, w_gate, w_up, w_down):
    ne = lax.axis_size("expert")
    ny = lax.axis_size("pipe") // 2
    toks, model = tokens.shape
    hidden = w_gate.shape[2]
    width = model // ny
    half = 16
    rows = ne * half
    far = ny // 2
    vmem = pl.BlockSpec(memory_space=pltpu.VMEM)
    hbm = pl.BlockSpec(memory_space=pl.ANY)
    dma = pltpu.SemaphoreType.DMA
    return pl.pallas_call(
        functools.partial(kernel, (ne, ny, half, width)),
        out_shape=jax.ShapeDtypeStruct((toks, width // 2), BF16),
        in_specs=[hbm, vmem, vmem, hbm, hbm, hbm],
        out_specs=vmem,
        scratch_shapes=[
            pltpu.VMEM((2, toks, width), BF16),
            pltpu.VMEM((2, rows, width), BF16),
            pltpu.VMEM((ny, 2 * rows, width), BF16),
            pltpu.VMEM((model, hidden), BF16),
            pltpu.VMEM((model, hidden), BF16),
            pltpu.VMEM((hidden, model), BF16),
            pltpu.VMEM((2 * rows, hidden), F32),
            pltpu.VMEM((2 * rows, hidden), F32),
            pltpu.VMEM((2 * rows, hidden), BF16),
            pltpu.VMEM((toks, 2 * rows), F32),
            pltpu.VMEM((ny, 2, rows, width), BF16),
            pltpu.VMEM((ny, rows, width), BF16),
            pltpu.VMEM((2, far, rows, width), BF16),
            pltpu.VMEM((2, far, rows, width), BF16),
            pltpu.VMEM((rows, width), BF16),
            pltpu.VMEM((rows, width), BF16),
            dma((5,)),
            dma((ne,)),
            dma((ne,)),
            dma((ne,)),
            dma((ne,)),
            dma((2, far, 2)),
            dma((2, far, 2)),
            dma((ny,)),
            dma((ny,)),
            dma((ny,)),
            dma((ny,)),
            dma((2, far, 2)),
            dma((2, far, 2)),
            dma((ne,)),
            dma((ne,)),
        ],
        compiler_params=pltpu.CompilerParams(
            collective_id=0, has_side_effects=True, vmem_limit_bytes=40 * 1024 * 1024
        ),
    )(tokens, routes, route_weights, w_gate, w_up, w_down)


def solution(mesh):
    return jax.shard_map(
        on_device,
        mesh=mesh,
        in_specs=(
            P(("dp", "expert"), None),
            P(("dp", "expert"), None),
            P(("dp", "expert"), None),
            P("expert", None, "pipe"),
            P("expert", None, "pipe"),
            P("expert", "pipe", None),
        ),
        out_specs=P(("dp", "expert"), "pipe"),
        check_vma=False,
    )
```

```python
import functools

import jax
import jax.numpy as jnp
from jax import lax
from jax.experimental import pallas as pl
from jax.experimental.pallas import tpu as pltpu
from jax.sharding import PartitionSpec as P

MESH = pl.DeviceIdType.MESH
F32 = jnp.float32
BF16 = jnp.bfloat16


def kernel(
    dims,
    tokens,
    routes,
    route_w,
    wg,
    wu,
    wd,
    out,
    route_v,
    weight_v,
    tok_v,
    xs,
    xbuf,
    wg_v,
    wu_v,
    wd_v,
    acc_g,
    acc_u,
    hid,
    mix,
    pk,
    cin,
    rin,
    rout,
    fin,
    rbuf,
    load_sem,
    xs_sem,
    xr_sem,
    os_sem,
    or_sem,
    ys_sem,
    yr_sem,
    cs_sem,
    cr_sem,
    ds_sem,
    dr_sem,
    rs_sem,
    rr_sem,
    fs_sem,
    fr_sem,
):
    ne, ny, half, width = dims
    rows = ne * half
    parts = 4
    sub = rows // parts
    pipe = lax.axis_index("pipe")
    e = lax.axis_index("expert")
    y = pipe // 2
    c = pipe % 2
    right = {"pipe": (y + 1) % ny * 2 + c}
    left = {"pipe": (y + ny - 1) % ny * 2 + c}
    peer = {"pipe": 2 * y + 1 - c}
    far = ny // 2
    hop = far - 1

    def chunk(j):
        return (y + j + ny) % ny

    def at16(x):
        return pl.multiple_of(x, 16)

    def remote(src, dst, send, recv, device):
        return pltpu.make_async_remote_copy(
            src_ref=src, dst_ref=dst, send_sem=send, recv_sem=recv, device_id=device, device_id_type=MESH
        )

    sent = []

    def go(copy):
        copy.start()
        sent.append(copy)

    barrier = pltpu.get_barrier_semaphore()
    for device in [{"expert": (e + j) % ne} for j in range(1, ne)] + [right, left, peer]:
        pl.semaphore_signal(barrier, inc=1, device_id=device, device_id_type=MESH)

    pairs = [(routes, route_v), (route_w, weight_v)]
    for i, j in enumerate((0, far)):
        cols = pl.ds(pl.multiple_of(chunk(j) * width, 128), width)
        pairs.append((tokens.at[:, cols], tok_v.at[i]))
    pairs += [(wg.at[0], wg_v), (wu.at[0], wu_v), (wd.at[0], wd_v)]
    loads = [pltpu.make_async_copy(src, dst, load_sem.at[i]) for i, (src, dst) in enumerate(pairs)]
    for copy in loads:
        copy.start()

    toks = tok_v.shape[1]
    row = lax.broadcasted_iota(jnp.int32, (2 * rows, toks), 0)
    hbits, rbits = half.bit_length() - 1, rows.bit_length() - 1
    expert_of = (row >> hbits) & (ne - 1)
    slot_of = ((row >> rbits) << hbits) + (row & (half - 1))
    loads[0].wait()
    loads[1].wait()
    first = route_v[0:1, :] == expert_of
    second = route_v[1:2, :] == expert_of
    named = jnp.logical_or(first, second)
    before = (
        lax.broadcasted_iota(jnp.int32, (toks, toks), 0) < lax.broadcasted_iota(jnp.int32, (toks, toks), 1)
    ).astype(F32)
    rank = jnp.dot(named.astype(F32).astype(BF16), before.astype(BF16), preferred_element_type=F32)
    taken = jnp.logical_and(named, rank == slot_of.astype(F32))
    mix[...] = jnp.where(taken, jnp.where(first, weight_v[0:1, :], weight_v[1:2, :]), 0.0)
    picked = taken.astype(F32)
    mine = jnp.where(c == 0, picked[:rows], picked[rows:]).astype(BF16)
    for i in range(2):
        loads[2 + i].wait()
        xs[i] = jnp.dot(mine, tok_v[i], preferred_element_type=F32).astype(BF16)

    pl.semaphore_wait(barrier, ne - 1 + 3)

    own_rows = pl.ds(at16(c * rows + e * half), half)
    far_first = sorted(range(1, ne), key=lambda n: -min(n, ne - n))
    for i, j, send, recv in ((0, 0, xs_sem, xr_sem), (1, far, os_sem, or_sem)):
        for n in far_first:
            t = (e + n) % ne
            go(
                remote(
                    xs.at[i, pl.ds(at16(t * half), half)],
                    xbuf.at[chunk(j), own_rows],
                    send.at[n],
                    recv.at[n],
                    {"expert": t},
                )
            )
        xbuf[chunk(j), own_rows, :] = xs[i, pl.ds(at16(e * half), half), :]

    def x_arrived(i, j, send, recv):
        for n in reversed(far_first):
            s = (e + ne - n) % ne
            where = pl.ds(at16(c * rows + s * half), half)
            remote(xs.at[i, pl.ds(0, half)], xbuf.at[chunk(j), where], send.at[n], recv.at[n], {"expert": s}).wait_recv()

    def y_copy(way, s, b, arriving=False):
        j = s + 1 if arriving else s
        ref = xbuf.at[chunk(-j if way == 0 else j), pl.ds(at16(c * rows + b * sub), sub)]
        return remote(ref, ref, ys_sem.at[way, s, b], yr_sem.at[way, s, b], right if way == 0 else left)

    def share(j, b=0, n=parts, core=c):
        i = j + hop
        ref = xbuf.at[chunk(j), pl.ds(at16(core * rows + b * sub), n * sub)]
        return remote(ref, ref, cs_sem.at[i, b], cr_sem.at[i, b], peer)

    def gemm(j, start=False):
        k = chunk(j)
        if hop == abs(j):
            for b in range(parts):
                share(j, b, 1, 1 - c).wait_recv()
        else:
            share(j, core=1 - c).wait_recv()
        lhs = xbuf[k]
        deep = pl.ds(pl.multiple_of(k * width, 128), width)
        for acc, w in ((acc_g, wg_v), (acc_u, wu_v)):
            term = jnp.dot(lhs, w[deep, :], preferred_element_type=F32)
            acc[...] = term if start else acc[...] + term

    x_arrived(0, 0, xs_sem, xr_sem)
    for b in range(parts):
        for way in range(2):
            go(y_copy(way, 0, b))
    go(share(0))
    for s in range(hop):
        for b in range(parts):
            for way in range(2):
                y_copy(way, s, b, True).wait_recv()
                if s + 1 < hop:
                    go(y_copy(way, s + 1, b))
                else:
                    go(share(-hop if way == 0 else hop, b, 1))
        if s + 1 < hop:
            go(share(-1 - s))
            go(share(s + 1))
        if s == 0:
            loads[4].wait()
            loads[5].wait()
            gemm(0, True)
        if s == 1:
            x_arrived(1, far, os_sem, or_sem)
            go(share(far))
        if s > 0:
            gemm(-s)
            gemm(s)
    gemm(far)
    gemm(-hop)
    gemm(hop)

    gate = acc_g[...]
    hid[...] = (gate / (1.0 + jnp.exp(-gate)) * acc_u[...]).astype(BF16)
    loads[6].wait()

    low = lax.broadcasted_iota(jnp.int32, (rows, width), 1) < width // 2

    def down(j):
        i = j + hop
        cols = pl.ds(pl.multiple_of(chunk(j) * width, 128), width)
        part = jnp.dot(hid[...], wd_v[:, cols], preferred_element_type=F32)
        a, b = part[:rows], part[rows:]
        pk[i, 0] = jnp.where(low, a, pltpu.roll(b, width // 2, 1)).astype(BF16)
        pk[i, 1] = jnp.where(low, pltpu.roll(a, width // 2, 1), b).astype(BF16)
        go(remote(pk.at[i, 1 - c], cin.at[i], ds_sem.at[i], dr_sem.at[i], peer))

    def met(j):
        i = j + hop
        remote(pk.at[i, 1 - c], cin.at[i], ds_sem.at[i], dr_sem.at[i], peer).wait_recv()

    def own(j, b):
        i = j + hop
        at = pl.ds(b * sub, sub)
        return pk[i, c, at, :].astype(F32) + cin[i, at, :].astype(F32)

    def r_copy(way, s, b):
        at = pl.ds(b * sub, sub)
        return remote(
            rout.at[way, s, at],
            rin.at[way, s, at],
            rs_sem.at[way, s, b],
            rr_sem.at[way, s, b],
            right if way == 0 else left,
        )

    def got(way, s, b):
        r_copy(way, s, b).wait_recv()
        return rin[way, s, pl.ds(b * sub, sub), :].astype(F32)

    def pass_on(way, s, b):
        if s == 0:
            total = own(far, b)
        else:
            total = own(far - s if way == 0 else s - far, b)
            if s > 1 or b // (parts // 2) == way:
                total = total + got(way, s - 1, b)
        rout[way, s, pl.ds(b * sub, sub), :] = total.astype(BF16)
        go(r_copy(way, s, b))

    down(far)
    for j in range(far - 1, max(0, far - 3), -1):
        down(j)
        down(-j)
    early, late = range(parts // 2), range(parts // 2, parts)
    met(far)
    for b in early:
        pass_on(0, 0, b)
        pass_on(1, 0, parts - 1 - b)
    met(far - 1)
    met(1 - far)
    for b in late:
        pass_on(0, 1, b)
        pass_on(1, 1, parts - 1 - b)
    for j in range(far - 3, 0, -1):
        down(j)
        down(-j)
    down(0)
    for b in early:
        pass_on(0, 1, b)
        pass_on(1, 1, parts - 1 - b)
    for s in range(2, far):
        met(far - s)
        met(s - far)
        for b in (*late, *early):
            pass_on(0, s, b)
            pass_on(1, s, parts - 1 - b)
    met(0)

    per = ne // parts
    own_back = pl.ds(at16(e * half), half)

    def back_copy(t):
        return remote(
            fin.at[pl.ds(t * half, half)], rbuf.at[own_back], fs_sem.at[t], fr_sem.at[e], {"expert": t}
        )

    order = [b for pair in zip(late, reversed(early)) for b in pair]
    for b in order:
        total = own(0, b) + got(0, far - 1, b) + got(1, far - 1, b)
        fin[pl.ds(b * sub, sub), :] = total.astype(BF16)
        for t in range(b * per, b * per + per):

            @pl.when(t != e)
            def _():
                back_copy(t).start()

    rbuf[own_back, :] = fin[own_back, :]
    weights = mix[...].T
    hi = weights.astype(BF16)
    lo = (weights - hi.astype(F32)).astype(BF16)
    for n in range(1, ne):
        t = (e + n) % ne
        at = pl.ds(at16(t * half), half)
        remote(fin.at[at], rbuf.at[at], fs_sem.at[t], fr_sem.at[t], {"expert": t}).wait()
    back = rbuf[...]

    def mixed(side):
        cols = slice(side * rows, side * rows + rows)
        return jnp.dot(hi[:, cols], back, preferred_element_type=F32) + jnp.dot(
            lo[:, cols], back, preferred_element_type=F32
        )

    total = mixed(0) + pltpu.roll(mixed(1), width // 2, 1)
    out[...] = total[:, : width // 2].astype(BF16)
    for copy in sent:
        copy.wait_send()


def on_device(tokens, routes, route_weights, w_gate, w_up, w_down):
    ne = lax.axis_size("expert")
    ny = lax.axis_size("pipe") // 2
    toks, model = tokens.shape
    hidden = w_gate.shape[2]
    width = model // ny
    half = 16
    rows = ne * half
    far = ny // 2
    vmem = pl.BlockSpec(memory_space=pltpu.VMEM)
    hbm = pl.BlockSpec(memory_space=pl.ANY)
    dma = pltpu.SemaphoreType.DMA
    return pl.pallas_call(
        functools.partial(kernel, (ne, ny, half, width)),
        out_shape=jax.ShapeDtypeStruct((toks, width // 2), BF16),
        in_specs=[hbm] * 6,
        out_specs=vmem,
        scratch_shapes=[
            pltpu.VMEM((2, toks), jnp.int32),
            pltpu.VMEM((2, toks), F32),
            pltpu.VMEM((2, toks, width), BF16),
            pltpu.VMEM((2, rows, width), BF16),
            pltpu.VMEM((ny, 2 * rows, width), BF16),
            pltpu.VMEM((model, hidden), BF16),
            pltpu.VMEM((model, hidden), BF16),
            pltpu.VMEM((hidden, model), BF16),
            pltpu.VMEM((2 * rows, hidden), F32),
            pltpu.VMEM((2 * rows, hidden), F32),
            pltpu.VMEM((2 * rows, hidden), BF16),
            pltpu.VMEM((2 * rows, toks), F32),
            pltpu.VMEM((ny, 2, rows, width), BF16),
            pltpu.VMEM((ny, rows, width), BF16),
            pltpu.VMEM((2, far, rows, width), BF16),
            pltpu.VMEM((2, far, rows, width), BF16),
            pltpu.VMEM((rows, width), BF16),
            pltpu.VMEM((rows, width), BF16),
            dma((7,)),
            dma((ne,)),
            dma((ne,)),
            dma((ne,)),
            dma((ne,)),
            dma((2, far, 4)),
            dma((2, far, 4)),
            dma((ny, 4)),
            dma((ny, 4)),
            dma((ny,)),
            dma((ny,)),
            dma((2, far, 4)),
            dma((2, far, 4)),
            dma((ne,)),
            dma((ne,)),
        ],
        compiler_params=pltpu.CompilerParams(
            collective_id=0, has_side_effects=True, vmem_limit_bytes=60 * 1024 * 1024
        ),
    )(tokens, routes.T, route_weights.T, w_gate, w_up, w_down)


def solution(mesh):
    return jax.shard_map(
        on_device,
        mesh=mesh,
        in_specs=(
            P(("dp", "expert"), None),
            P(("dp", "expert"), None),
            P(("dp", "expert"), None),
            P("expert", None, "pipe"),
            P("expert", None, "pipe"),
            P("expert", "pipe", None),
        ),
        out_specs=P(("dp", "expert"), "pipe"),
        check_vma=False,
    )
```

```python
import functools

import jax
import jax.numpy as jnp
from jax import lax
from jax.experimental import pallas as pl
from jax.experimental.pallas import tpu as pltpu
from jax.sharding import PartitionSpec as P

MESH = pl.DeviceIdType.MESH
F32 = jnp.float32
BF16 = jnp.bfloat16


def kernel(
    dims,
    tokens,
    routes,
    route_w,
    wg,
    wu,
    wd,
    out,
    route_v,
    weight_v,
    tok_v,
    xs,
    xbuf,
    wg_v,
    wu_v,
    wd_v,
    acc_g,
    acc_u,
    hid,
    mix,
    pk,
    cin,
    rin,
    rout,
    fin,
    rbuf,
    load_sem,
    xs_sem,
    xr_sem,
    ys_sem,
    yr_sem,
    cs_sem,
    cr_sem,
    ds_sem,
    dr_sem,
    rs_sem,
    rr_sem,
    fs_sem,
    fr_sem,
    ready,
):
    ne, ny, half, width = dims
    rows = ne * half
    parts = 4
    sub = rows // parts
    pipe = lax.axis_index("pipe")
    e = lax.axis_index("expert")
    y = pipe // 2
    c = pipe % 2
    d = lax.axis_index("dp")
    far = ny // 2
    hop = far - 1
    steps = far - 2

    def zero(v, n):
        return 1 - (v + n - 1) // n

    def carrier(at_y, at_e, h):
        if h == 1:
            return 1
        return zero(d, lax.axis_size("dp")) * zero(at_y, ny) * zero(at_e, ne)

    def chip(at_y, h):
        at_y = (at_y + ny) % ny
        return {"pipe": 2 * at_y + carrier(at_y, e, h)}

    def across(t, h):
        return {"pipe": 2 * y + carrier(y, t, h), "expert": t}

    right = {"pipe": (y + 1) % ny * 2 + c}
    left = {"pipe": (y + ny - 1) % ny * 2 + c}
    peer = {"pipe": 2 * y + 1 - c}
    front = d == 0
    lone = jnp.logical_and(front, jnp.logical_and(pipe == 0, e == 0))
    double = jnp.logical_and(front, jnp.logical_and(pipe == 1, e == 0))
    in_row = jnp.logical_and(y == 0, e != 0)
    in_column = jnp.logical_and(e == 0, jnp.logical_or(y == 1, y == ny - 1))
    beside = jnp.logical_and(jnp.logical_and(front, c == 0), jnp.logical_or(in_row, in_column))
    active = [carrier(y, e, h) == c for h in range(2)]

    def chunk(j):
        return (y + j + ny) % ny

    def at16(x):
        return pl.multiple_of(x, 16)

    def remote(src, dst, send, recv, device):
        return pltpu.make_async_remote_copy(
            src_ref=src, dst_ref=dst, send_sem=send, recv_sem=recv, device_id=device, device_id_type=MESH
        )

    sent = []
    sent_of = [[], []]

    def go(copy):
        copy.start()
        sent.append(copy)

    def send(h, make):
        make().start()
        sent_of[h].append(make)

    def carry(work):
        for h in range(2):

            @pl.when(active[h])
            def _():
                work(h)

    barrier = pltpu.get_barrier_semaphore()

    def greet(semaphore, device):
        pl.semaphore_signal(semaphore, inc=1, device_id=device, device_id_type=MESH)

    neighbours = [{"expert": (e + j) % ne} for j in range(1, ne)] + [right, left, peer]

    @pl.when(jnp.logical_not(lone))
    def _():
        for device in neighbours:
            greet(barrier, device)

    @pl.when(double)
    def _():
        for device in [{"pipe": 0, "expert": t} for t in range(1, ne)] + [{"pipe": 2}, {"pipe": 2 * ny - 2}]:
            greet(barrier, device)

    @pl.when(beside)
    def _():
        greet(barrier, {"pipe": 1, "expert": 0})

    pairs = [(routes, route_v), (route_w, weight_v)]
    direct = [0, far] + [j for k in range(steps + 1, far) for j in (-k, k)]
    for i, j in enumerate(direct):
        cols = pl.ds(pl.multiple_of(chunk(j) * width, 128), width)
        pairs.append((tokens.at[:, cols], tok_v.at[i]))
    pairs += [(wg.at[0], wg_v), (wu.at[0], wu_v), (wd.at[0], wd_v)]
    loads = [pltpu.make_async_copy(src, dst, load_sem.at[i]) for i, (src, dst) in enumerate(pairs)]
    for copy in loads:
        copy.start()

    toks = tok_v.shape[1]
    row = lax.broadcasted_iota(jnp.int32, (2 * rows, toks), 0)
    hbits, rbits = half.bit_length() - 1, rows.bit_length() - 1
    expert_of = (row >> hbits) & (ne - 1)
    slot_of = ((row >> rbits) << hbits) + (row & (half - 1))
    loads[0].wait()
    loads[1].wait()
    first = route_v[0:1, :] == expert_of
    second = route_v[1:2, :] == expert_of
    named = jnp.logical_or(first, second)
    before = (
        lax.broadcasted_iota(jnp.int32, (toks, toks), 0) < lax.broadcasted_iota(jnp.int32, (toks, toks), 1)
    ).astype(F32)
    rank = jnp.dot(named.astype(F32).astype(BF16), before.astype(BF16), preferred_element_type=F32)
    taken = jnp.logical_and(named, rank == slot_of.astype(F32))
    mix[...] = jnp.where(taken, jnp.where(first, weight_v[0:1, :], weight_v[1:2, :]), 0.0)
    picked = taken.astype(F32)
    picked = picked.astype(BF16)
    loads[2].wait()
    xs[0] = jnp.dot(picked, tok_v[0], preferred_element_type=F32).astype(BF16)

    @pl.when(jnp.logical_not(double))
    def _():
        pl.semaphore_wait(barrier, len(neighbours))

    @pl.when(double)
    def _():
        pl.semaphore_wait(barrier, 2 * len(neighbours) - 2)

    @pl.when(lone)
    def _():
        for device in neighbours:
            greet(ready, device)

    far_first = sorted(range(1, ne), key=lambda n: -min(n, ne - n))

    def slab(core, t):
        return pl.ds(at16(core * rows + t * half), half)

    def x_copy(h, i, n):
        t = (e + n) % ne
        return remote(
            xs.at[i, slab(h, t)],
            xbuf.at[chunk(direct[i]), slab(h, e)],
            xs_sem.at[h, i, n],
            xr_sem.at[h, i, n],
            across(t, h),
        )

    def x_send(h, i):
        for n in far_first:
            send(h, functools.partial(x_copy, h, i, n))
        xbuf[chunk(direct[i]), slab(h, e), :] = xs[i, slab(h, e), :]

    def x_arrived(h, i):
        for n in reversed(far_first):
            t = (e + ne - n) % ne
            remote(
                xs.at[i, slab(h, 0)],
                xbuf.at[chunk(direct[i]), slab(h, t)],
                xs_sem.at[h, i, n],
                xr_sem.at[h, i, n],
                across(t, h),
            ).wait_recv()

    def y_copy(h, way, s, b, arriving=False):
        j = s + 1 if arriving else s
        ref = xbuf.at[chunk(-j if way == 0 else j), pl.ds(h * rows + b * sub, sub)]
        return remote(
            ref, ref, ys_sem.at[h, way, s, b], yr_sem.at[h, way, s, b], chip(y + 1 if way == 0 else y - 1, h)
        )

    def share_copy(h, j):
        ref = xbuf.at[chunk(j), pl.ds(h * rows, rows)]
        return remote(ref, ref, cs_sem.at[h, j + hop], cr_sem.at[h, j + hop], peer)

    def share(h, *chunks):
        for j in chunks:
            send(h, functools.partial(share_copy, h, j))

    def gemm(j, start=False):
        k = chunk(j)
        for h in range(2):

            @pl.when(jnp.logical_not(active[h]))
            def _():
                share_copy(h, j).wait_recv()

        lhs = xbuf[k]
        deep = pl.ds(pl.multiple_of(k * width, 128), width)
        for acc, w in ((acc_g, wg_v), (acc_u, wu_v)):
            term = jnp.dot(lhs, w[deep, :], preferred_element_type=F32)
            acc[...] = term if start else acc[...] + term

    carry(lambda h: x_send(h, 0))
    for i in range(1, len(direct)):
        loads[2 + i].wait()
        xs[i] = jnp.dot(picked, tok_v[i], preferred_element_type=F32).astype(BF16)
        carry(lambda h: x_send(h, i))

    def first_hop(h):
        x_arrived(h, 0)
        for b in range(parts):
            for way in range(2):
                send(h, functools.partial(y_copy, h, way, 0, b))

    def next_hop(s, h):
        for b in range(parts):
            for way in range(2):
                y_copy(h, way, s, b, True).wait_recv()
                if s + 1 < steps:
                    send(h, functools.partial(y_copy, h, way, s + 1, b))

    def x_rest(h, i):
        x_arrived(h, i)
        share(h, direct[i])

    def last_hop(h):
        next_hop(steps - 1, h)
        share(h, -steps, steps)

    carry(first_hop)

    @pl.when(jnp.logical_not(jnp.logical_or(double, lone)))
    def _():
        for h in range(2):

            @pl.when(active[h])
            def _():
                share_copy(h, 0).start()

    for s in range(steps - 1):
        carry(functools.partial(next_hop, s))

    @pl.when(double)
    def _():
        pl.semaphore_wait(ready, 1)
        share_copy(0, 0).start()
        share_copy(1, 0).start()

    for h in range(2):
        sent_of[h].append(functools.partial(share_copy, h, 0))
    carry(lambda h: share(h, *[j for k in range(1, steps) for j in (-k, k)]))
    ahead = len(pairs) - 3
    loads[ahead].wait()
    loads[ahead + 1].wait()
    gemm(0, True)
    carry(lambda h: x_rest(h, 1))
    for k in range(1, steps):
        gemm(-k)
        gemm(k)
    carry(last_hop)
    for i in range(2, len(direct)):
        carry(lambda h: x_rest(h, i))
    gemm(far)
    for k in range(steps, far):
        gemm(-k)
        gemm(k)

    @pl.when(beside)
    def _():
        pl.semaphore_wait(ready, 1)

    gate = acc_g[...]
    hid[...] = (gate / (1.0 + jnp.exp(-gate)) * acc_u[...]).astype(BF16)
    loads[ahead + 2].wait()

    low = lax.broadcasted_iota(jnp.int32, (rows, width), 1) < width // 2

    def down(j):
        i = j + hop
        cols = pl.ds(pl.multiple_of(chunk(j) * width, 128), width)
        part = jnp.dot(hid[...], wd_v[:, cols], preferred_element_type=F32)
        a, b = part[:rows], part[rows:]
        pk[i, 0] = jnp.where(low, a, pltpu.roll(b, width // 2, 1)).astype(BF16)
        pk[i, 1] = jnp.where(low, pltpu.roll(a, width // 2, 1), b).astype(BF16)
        go(remote(pk.at[i, 1 - c], cin.at[i], ds_sem.at[i], dr_sem.at[i], peer))

    def met(j):
        i = j + hop
        remote(pk.at[i, 1 - c], cin.at[i], ds_sem.at[i], dr_sem.at[i], peer).wait_recv()

    def own(j, b):
        i = j + hop
        at = pl.ds(b * sub, sub)
        return pk[i, c, at, :].astype(F32) + cin[i, at, :].astype(F32)

    def r_copy(way, s, b):
        at = pl.ds(b * sub, sub)
        return remote(
            rout.at[way, s, at],
            rin.at[way, s, at],
            rs_sem.at[way, s, b],
            rr_sem.at[way, s, b],
            right if way == 0 else left,
        )

    def got(way, s, b):
        r_copy(way, s, b).wait_recv()
        return rin[way, s, pl.ds(b * sub, sub), :].astype(F32)

    def pass_on(way, s, b):
        if s == 0:
            total = own(far, b)
        else:
            total = own(far - s if way == 0 else s - far, b)
            if s > 1 or b // (parts // 2) == way:
                total = total + got(way, s - 1, b)
        rout[way, s, pl.ds(b * sub, sub), :] = total.astype(BF16)
        go(r_copy(way, s, b))

    down(far)
    for j in range(far - 1, max(0, far - 3), -1):
        down(j)
        down(-j)
    early, late = range(parts // 2), range(parts // 2, parts)
    met(far)
    for b in early:
        pass_on(0, 0, b)
        pass_on(1, 0, parts - 1 - b)
    met(far - 1)
    met(1 - far)
    for b in late:
        pass_on(0, 1, b)
        pass_on(1, 1, parts - 1 - b)
    for j in range(far - 3, 0, -1):
        down(j)
        down(-j)
    down(0)
    for b in early:
        pass_on(0, 1, b)
        pass_on(1, 1, parts - 1 - b)
    for s in range(2, far):
        met(far - s)
        met(s - far)
        for b in (*late, *early):
            pass_on(0, s, b)
            pass_on(1, s, parts - 1 - b)
    met(0)

    per = ne // parts
    own_back = pl.ds(at16(e * half), half)

    def back_copy(t):
        return remote(
            fin.at[pl.ds(t * half, half)], rbuf.at[own_back], fs_sem.at[t], fr_sem.at[e], {"expert": t}
        )

    order = [b for pair in zip(late, reversed(early)) for b in pair]
    for b in order:
        total = own(0, b) + got(0, far - 1, b) + got(1, far - 1, b)
        fin[pl.ds(b * sub, sub), :] = total.astype(BF16)
        for t in range(b * per, b * per + per):

            @pl.when(t != e)
            def _():
                back_copy(t).start()

    rbuf[own_back, :] = fin[own_back, :]
    weights = mix[...].T
    hi = weights.astype(BF16)
    lo = (weights - hi.astype(F32)).astype(BF16)
    for n in range(1, ne):
        t = (e + n) % ne
        at = pl.ds(at16(t * half), half)
        remote(fin.at[at], rbuf.at[at], fs_sem.at[t], fr_sem.at[t], {"expert": t}).wait()
    back = rbuf[...]

    def mixed(side):
        cols = slice(side * rows, side * rows + rows)
        return jnp.dot(hi[:, cols], back, preferred_element_type=F32) + jnp.dot(
            lo[:, cols], back, preferred_element_type=F32
        )

    total = mixed(0) + pltpu.roll(mixed(1), width // 2, 1)
    out[...] = total[:, : width // 2].astype(BF16)
    for copy in sent:
        copy.wait_send()
    carry(lambda h: [make().wait_send() for make in sent_of[h]])


def on_device(tokens, routes, route_weights, w_gate, w_up, w_down):
    ne = lax.axis_size("expert")
    ny = lax.axis_size("pipe") // 2
    toks, model = tokens.shape
    hidden = w_gate.shape[2]
    width = model // ny
    half = 16
    rows = ne * half
    far = ny // 2
    vmem = pl.BlockSpec(memory_space=pltpu.VMEM)
    hbm = pl.BlockSpec(memory_space=pl.ANY)
    dma = pltpu.SemaphoreType.DMA
    return pl.pallas_call(
        functools.partial(kernel, (ne, ny, half, width)),
        out_shape=jax.ShapeDtypeStruct((toks, width // 2), BF16),
        in_specs=[hbm] * 6,
        out_specs=vmem,
        scratch_shapes=[
            pltpu.VMEM((2, toks), jnp.int32),
            pltpu.VMEM((2, toks), F32),
            pltpu.VMEM((4, toks, width), BF16),
            pltpu.VMEM((4, 2 * rows, width), BF16),
            pltpu.VMEM((ny, 2 * rows, width), BF16),
            pltpu.VMEM((model, hidden), BF16),
            pltpu.VMEM((model, hidden), BF16),
            pltpu.VMEM((hidden, model), BF16),
            pltpu.VMEM((2 * rows, hidden), F32),
            pltpu.VMEM((2 * rows, hidden), F32),
            pltpu.VMEM((2 * rows, hidden), BF16),
            pltpu.VMEM((2 * rows, toks), F32),
            pltpu.VMEM((ny, 2, rows, width), BF16),
            pltpu.VMEM((ny, rows, width), BF16),
            pltpu.VMEM((2, far, rows, width), BF16),
            pltpu.VMEM((2, far, rows, width), BF16),
            pltpu.VMEM((rows, width), BF16),
            pltpu.VMEM((rows, width), BF16),
            dma((9,)),
            dma((2, 4, ne)),
            dma((2, 4, ne)),
            dma((2, 2, far - 2, 4)),
            dma((2, 2, far - 2, 4)),
            dma((2, ny)),
            dma((2, ny)),
            dma((ny,)),
            dma((ny,)),
            dma((2, far, 4)),
            dma((2, far, 4)),
            dma((ne,)),
            dma((ne,)),
            pltpu.SemaphoreType.REGULAR,
        ],
        compiler_params=pltpu.CompilerParams(
            collective_id=0, has_side_effects=True, vmem_limit_bytes=60 * 1024 * 1024
        ),
    )(tokens, routes.T, route_weights.T, w_gate, w_up, w_down)


def solution(mesh):
    return jax.shard_map(
        on_device,
        mesh=mesh,
        in_specs=(
            P(("dp", "expert"), None),
            P(("dp", "expert"), None),
            P(("dp", "expert"), None),
            P("expert", None, "pipe"),
            P("expert", None, "pipe"),
            P("expert", "pipe", None),
        ),
        out_specs=P(("dp", "expert"), "pipe"),
        check_vma=False,
    )
```

```python
import functools

import jax
import jax.numpy as jnp
from jax import lax
from jax.experimental import pallas as pl
from jax.experimental.pallas import tpu as pltpu
from jax.sharding import PartitionSpec as P

MESH = pl.DeviceIdType.MESH
F32 = jnp.float32
BF16 = jnp.bfloat16


def kernel(
    dims,
    tokens,
    routes,
    route_w,
    wg,
    wu,
    wd,
    out,
    route_v,
    weight_v,
    tok_v,
    xs,
    xbuf,
    wg_v,
    wu_v,
    wd_v,
    acc_g,
    acc_u,
    hid,
    mix,
    pk,
    cin,
    rin,
    rin_o,
    rout,
    fin,
    rbuf,
    load_sem,
    xs_sem,
    xr_sem,
    ys_sem,
    yr_sem,
    cs_sem,
    cr_sem,
    ds_sem,
    dr_sem,
    rs_sem,
    rr_sem,
    fs_sem,
    fr_sem,
    ts_sem,
    tr_sem,
    os_sem,
    or_sem,
    ready,
):
    ne, ny, half, width = dims
    rows = ne * half
    parts = 4
    sub = rows // parts
    pipe = lax.axis_index("pipe")
    e = lax.axis_index("expert")
    y = pipe // 2
    c = pipe % 2
    d = lax.axis_index("dp")
    far = ny // 2
    hop = far - 1
    steps = far - 2

    def zero(v, n):
        return 1 - (v + n - 1) // n

    def carrier(at_y, at_e, h):
        if h == 1:
            return 1
        return zero(d, lax.axis_size("dp")) * zero(at_y, ny) * zero(at_e, ne)

    def chip(at_y, h):
        at_y = (at_y + ny) % ny
        return {"pipe": 2 * at_y + carrier(at_y, e, h)}

    def across(t, h):
        return {"pipe": 2 * y + carrier(y, t, h), "expert": t}

    right = {"pipe": (y + 1) % ny * 2 + c}
    left = {"pipe": (y + ny - 1) % ny * 2 + c}
    peer = {"pipe": 2 * y + 1 - c}
    slant = [{"pipe": (y + 1) % ny * 2 + 1 - c}, {"pipe": (y + ny - 1) % ny * 2 + 1 - c}]
    front = d == 0
    lone = jnp.logical_and(front, jnp.logical_and(pipe == 0, e == 0))
    double = jnp.logical_and(front, jnp.logical_and(pipe == 1, e == 0))
    in_row = jnp.logical_and(jnp.logical_and(front, pipe == 0), e != 0)
    column = jnp.logical_and(jnp.logical_and(front, e == 0), jnp.logical_or(y == 1, y == ny - 1))
    active = [carrier(y, e, h) == c for h in range(2)]

    def chunk(j):
        return (y + j + ny) % ny

    def at16(x):
        return pl.multiple_of(x, 16)

    def remote(src, dst, send, recv, device):
        return pltpu.make_async_remote_copy(
            src_ref=src, dst_ref=dst, send_sem=send, recv_sem=recv, device_id=device, device_id_type=MESH
        )

    sent = []
    sent_of = [[], []]

    def go(copy):
        copy.start()
        sent.append(copy)

    def send(h, make):
        make().start()
        sent_of[h].append(make)

    def carry(work):
        for h in range(2):

            @pl.when(active[h])
            def _():
                work(h)

    barrier = pltpu.get_barrier_semaphore()

    def greet(semaphore, device):
        pl.semaphore_signal(semaphore, inc=1, device_id=device, device_id_type=MESH)

    neighbours = [{"expert": (e + j) % ne} for j in range(1, ne)] + [right, left, peer, *slant]

    @pl.when(jnp.logical_not(lone))
    def _():
        for device in neighbours:
            greet(barrier, device)

    @pl.when(double)
    def _():
        for t in range(1, ne):
            greet(barrier, {"pipe": 0, "expert": t})

    @pl.when(in_row)
    def _():
        greet(barrier, {"pipe": 1, "expert": 0})

    pairs = [(routes, route_v), (route_w, weight_v)]
    direct = [0, far] + [j for k in range(steps + 1, far) for j in (-k, k)]
    for i, j in enumerate(direct):
        cols = pl.ds(pl.multiple_of(chunk(j) * width, 128), width)
        pairs.append((tokens.at[:, cols], tok_v.at[i]))
    pairs += [(wg.at[0], wg_v), (wu.at[0], wu_v), (wd.at[0], wd_v)]
    loads = [pltpu.make_async_copy(src, dst, load_sem.at[i]) for i, (src, dst) in enumerate(pairs)]
    for copy in loads:
        copy.start()

    toks = tok_v.shape[1]
    row = lax.broadcasted_iota(jnp.int32, (2 * rows, toks), 0)
    hbits, rbits = half.bit_length() - 1, rows.bit_length() - 1
    expert_of = (row >> hbits) & (ne - 1)
    slot_of = ((row >> rbits) << hbits) + (row & (half - 1))
    loads[0].wait()
    loads[1].wait()
    first = route_v[0:1, :] == expert_of
    second = route_v[1:2, :] == expert_of
    named = jnp.logical_or(first, second)
    before = (
        lax.broadcasted_iota(jnp.int32, (toks, toks), 0) < lax.broadcasted_iota(jnp.int32, (toks, toks), 1)
    ).astype(F32)
    rank = jnp.dot(named.astype(F32).astype(BF16), before.astype(BF16), preferred_element_type=F32)
    taken = jnp.logical_and(named, rank == slot_of.astype(F32))
    mix[...] = jnp.where(taken, jnp.where(first, weight_v[0:1, :], weight_v[1:2, :]), 0.0)
    picked = taken.astype(F32)
    picked = picked.astype(BF16)
    loads[2].wait()
    xs[0] = jnp.dot(picked, tok_v[0], preferred_element_type=F32).astype(BF16)

    @pl.when(jnp.logical_not(jnp.logical_or(double, column)))
    def _():
        pl.semaphore_wait(barrier, len(neighbours))

    @pl.when(column)
    def _():
        pl.semaphore_wait(barrier, len(neighbours) - 1)

    @pl.when(double)
    def _():
        pl.semaphore_wait(barrier, len(neighbours) + ne - 2)

    @pl.when(lone)
    def _():
        for device in neighbours:
            greet(ready, device)

    far_first = sorted(range(1, ne), key=lambda n: -min(n, ne - n))

    def slab(core, t):
        return pl.ds(at16(core * rows + t * half), half)

    def x_copy(h, i, n):
        t = (e + n) % ne
        return remote(
            xs.at[i, slab(h, t)],
            xbuf.at[chunk(direct[i]), slab(h, e)],
            xs_sem.at[h, i, n],
            xr_sem.at[h, i, n],
            across(t, h),
        )

    def x_send(h, i):
        for n in far_first:
            send(h, functools.partial(x_copy, h, i, n))
        xbuf[chunk(direct[i]), slab(h, e), :] = xs[i, slab(h, e), :]

    def x_arrived(h, i):
        for n in reversed(far_first):
            t = (e + ne - n) % ne
            remote(
                xs.at[i, slab(h, 0)],
                xbuf.at[chunk(direct[i]), slab(h, t)],
                xs_sem.at[h, i, n],
                xr_sem.at[h, i, n],
                across(t, h),
            ).wait_recv()

    def y_copy(h, way, s, b, arriving=False):
        j = s + 1 if arriving else s
        ref = xbuf.at[chunk(-j if way == 0 else j), pl.ds(h * rows + b * sub, sub)]
        return remote(
            ref, ref, ys_sem.at[h, way, s, b], yr_sem.at[h, way, s, b], chip(y + 1 if way == 0 else y - 1, h)
        )

    to_open = [
        jnp.logical_not(jnp.logical_and(jnp.logical_and(front, e == 0), (y + step + ny) % ny == 0)) for step in (1, -1)
    ]

    def twin_copy(h, way, b, arriving=False):
        j = steps if arriving else steps - 1
        ref = xbuf.at[chunk(-j if way == 0 else j), pl.ds(h * rows + b * sub, sub)]
        at_y = (y + (1 if way == 0 else -1) + ny) % ny
        return remote(ref, ref, ts_sem.at[h, way, b], tr_sem.at[h, way, b], {"pipe": 2 * at_y + 1 - h})

    def share_copy(h, j):
        ref = xbuf.at[chunk(j), pl.ds(h * rows, rows)]
        return remote(ref, ref, cs_sem.at[h, j + hop], cr_sem.at[h, j + hop], peer)

    def share(h, *chunks):
        for j in chunks:
            send(h, functools.partial(share_copy, h, j))

    def gemm(j, start=False):
        k = chunk(j)
        for h in range(2):

            if abs(j) == steps:

                @pl.when(jnp.logical_not(jnp.logical_or(active[h], lone)))
                def _():
                    for b in range(parts):
                        twin_copy(h, 0 if j < 0 else 1, b, True).wait_recv()

                @pl.when(lone)
                def _():
                    share_copy(h, j).wait_recv()

            else:

                @pl.when(jnp.logical_not(active[h]))
                def _():
                    share_copy(h, j).wait_recv()

        lhs = xbuf[k]
        deep = pl.ds(pl.multiple_of(k * width, 128), width)
        for acc, w in ((acc_g, wg_v), (acc_u, wu_v)):
            term = jnp.dot(lhs, w[deep, :], preferred_element_type=F32)
            acc[...] = term if start else acc[...] + term

    carry(lambda h: x_send(h, 0))
    for i in range(1, len(direct)):
        loads[2 + i].wait()
        xs[i] = jnp.dot(picked, tok_v[i], preferred_element_type=F32).astype(BF16)
        carry(lambda h: x_send(h, i))

    def first_hop(h):
        x_arrived(h, 0)
        for b in range(parts):
            for way in range(2):
                send(h, functools.partial(y_copy, h, way, 0, b))

    def next_hop(s, h):
        for b in range(parts):
            for way in range(2):
                y_copy(h, way, s, b, True).wait_recv()
                if s + 1 < steps:
                    send(h, functools.partial(y_copy, h, way, s + 1, b))
                if s + 2 == steps:

                    @pl.when(to_open[way])
                    def _():
                        twin_copy(h, way, b).start()

    def x_rest(h, i):
        x_arrived(h, i)
        share(h, direct[i])

    def last_hop(h):
        next_hop(steps - 1, h)

        @pl.when(double)
        def _():
            share_copy(h, -steps).start()
            share_copy(h, steps).start()

    carry(first_hop)

    @pl.when(jnp.logical_not(jnp.logical_or(double, lone)))
    def _():
        for h in range(2):

            @pl.when(active[h])
            def _():
                share_copy(h, 0).start()

    for s in range(steps - 1):
        carry(functools.partial(next_hop, s))

    @pl.when(double)
    def _():
        pl.semaphore_wait(ready, 1)
        share_copy(0, 0).start()
        share_copy(1, 0).start()

    for h in range(2):
        sent_of[h].append(functools.partial(share_copy, h, 0))
    carry(lambda h: share(h, *[j for k in range(1, steps) for j in (-k, k)]))
    ahead = len(pairs) - 3
    loads[ahead].wait()
    loads[ahead + 1].wait()
    gemm(0, True)
    carry(lambda h: x_rest(h, 1))
    for k in range(1, steps):
        gemm(-k)
        gemm(k)
    carry(last_hop)
    for i in range(2, len(direct)):
        carry(lambda h: x_rest(h, i))
    gemm(far)
    for k in range(steps, far):
        gemm(-k)
        gemm(k)

    @pl.when(jnp.logical_or(in_row, column))
    def _():
        pl.semaphore_wait(ready, 1)

    gate = acc_g[...]
    hid[...] = (gate / (1.0 + jnp.exp(-gate)) * acc_u[...]).astype(BF16)
    loads[ahead + 2].wait()

    low = lax.broadcasted_iota(jnp.int32, (rows, width), 1) < width // 2

    def down(j):
        i = j + hop
        cols = pl.ds(pl.multiple_of(chunk(j) * width, 128), width)
        part = jnp.dot(hid[...], wd_v[:, cols], preferred_element_type=F32)
        a, b = part[:rows], part[rows:]
        pk[i, 0] = jnp.where(low, a, pltpu.roll(b, width // 2, 1)).astype(BF16)
        pk[i, 1] = jnp.where(low, pltpu.roll(a, width // 2, 1), b).astype(BF16)
        if j != far:
            go(remote(pk.at[i, 1 - c], cin.at[i], ds_sem.at[i], dr_sem.at[i], peer))

    def met(j):
        i = j + hop
        remote(pk.at[i, 1 - c], cin.at[i], ds_sem.at[i], dr_sem.at[i], peer).wait_recv()

    def own(j, b):
        i = j + hop
        at = pl.ds(b * sub, sub)
        return pk[i, c, at, :].astype(F32) + cin[i, at, :].astype(F32)

    def r_copy(way, s, b):
        at = pl.ds(b * sub, sub)
        return remote(
            rout.at[way, s, at],
            rin.at[way, s, at],
            rs_sem.at[way, s, b],
            rr_sem.at[way, s, b],
            right if way == 0 else left,
        )

    def got(way, s, b):
        r_copy(way, s, b).wait_recv()
        return rin[way, s, pl.ds(b * sub, sub), :].astype(F32)

    def first_copy(way, b, other):
        at = pl.ds(b * sub, sub)
        if other:
            return remote(
                pk.at[far + hop, 1 - c, at], rin_o.at[way, at], os_sem.at[way, b], or_sem.at[way, b], slant[way]
            )
        return remote(
            pk.at[far + hop, c, at],
            rin.at[way, 0, at],
            rs_sem.at[way, 0, b],
            rr_sem.at[way, 0, b],
            right if way == 0 else left,
        )

    def got_first(way, b):
        first_copy(way, b, True).wait_recv()
        return got(way, 0, b) + rin_o[way, pl.ds(b * sub, sub), :].astype(F32)

    def pass_on(way, s, b):
        total = own(far - s if way == 0 else s - far, b)
        if s > 1:
            total = total + got(way, s - 1, b)
        elif b // (parts // 2) == way:
            total = total + got_first(way, b)
        rout[way, s, pl.ds(b * sub, sub), :] = total.astype(BF16)
        go(r_copy(way, s, b))

    down(far)
    early, late = range(parts // 2), range(parts // 2, parts)
    for b in early:
        for other in (True, False):
            go(first_copy(0, b, other))
            go(first_copy(1, parts - 1 - b, other))
    for j in range(far - 1, max(0, far - 3), -1):
        down(j)
        down(-j)
    met(far - 1)
    met(1 - far)
    for b in late:
        pass_on(0, 1, b)
        pass_on(1, 1, parts - 1 - b)
    for j in range(far - 3, 0, -1):
        down(j)
        down(-j)
    down(0)
    for b in early:
        pass_on(0, 1, b)
        pass_on(1, 1, parts - 1 - b)
    for s in range(2, far):
        met(far - s)
        met(s - far)
        for b in (*late, *early):
            pass_on(0, s, b)
            pass_on(1, s, parts - 1 - b)
    met(0)

    per = ne // parts
    own_back = pl.ds(at16(e * half), half)

    def back_copy(t):
        return remote(
            fin.at[pl.ds(t * half, half)], rbuf.at[own_back], fs_sem.at[t], fr_sem.at[e], {"expert": t}
        )

    order = [b for pair in zip(late, reversed(early)) for b in pair]
    for b in order:
        total = own(0, b) + got(0, far - 1, b) + got(1, far - 1, b)
        fin[pl.ds(b * sub, sub), :] = total.astype(BF16)
        for t in range(b * per, b * per + per):

            @pl.when(t != e)
            def _():
                back_copy(t).start()

    rbuf[own_back, :] = fin[own_back, :]
    weights = mix[...].T
    hi = weights.astype(BF16)
    lo = (weights - hi.astype(F32)).astype(BF16)
    for n in range(1, ne):
        t = (e + n) % ne
        at = pl.ds(at16(t * half), half)
        remote(fin.at[at], rbuf.at[at], fs_sem.at[t], fr_sem.at[t], {"expert": t}).wait()
    back = rbuf[...]

    def mixed(side):
        cols = slice(side * rows, side * rows + rows)
        return jnp.dot(hi[:, cols], back, preferred_element_type=F32) + jnp.dot(
            lo[:, cols], back, preferred_element_type=F32
        )

    total = mixed(0) + pltpu.roll(mixed(1), width // 2, 1)
    out[...] = total[:, : width // 2].astype(BF16)
    for copy in sent:
        copy.wait_send()

    def sent_all(h):
        for make in sent_of[h]:
            make().wait_send()
        for way in range(2):

            @pl.when(to_open[way])
            def _():
                for b in range(parts):
                    twin_copy(h, way, b).wait_send()

        @pl.when(double)
        def _():
            share_copy(h, -steps).wait_send()
            share_copy(h, steps).wait_send()

    carry(sent_all)


def on_device(tokens, routes, route_weights, w_gate, w_up, w_down):
    ne = lax.axis_size("expert")
    ny = lax.axis_size("pipe") // 2
    toks, model = tokens.shape
    hidden = w_gate.shape[2]
    width = model // ny
    half = 16
    rows = ne * half
    far = ny // 2
    vmem = pl.BlockSpec(memory_space=pltpu.VMEM)
    hbm = pl.BlockSpec(memory_space=pl.ANY)
    dma = pltpu.SemaphoreType.DMA
    return pl.pallas_call(
        functools.partial(kernel, (ne, ny, half, width)),
        out_shape=jax.ShapeDtypeStruct((toks, width // 2), BF16),
        in_specs=[hbm] * 6,
        out_specs=vmem,
        scratch_shapes=[
            pltpu.VMEM((2, toks), jnp.int32),
            pltpu.VMEM((2, toks), F32),
            pltpu.VMEM((4, toks, width), BF16),
            pltpu.VMEM((4, 2 * rows, width), BF16),
            pltpu.VMEM((ny, 2 * rows, width), BF16),
            pltpu.VMEM((model, hidden), BF16),
            pltpu.VMEM((model, hidden), BF16),
            pltpu.VMEM((hidden, model), BF16),
            pltpu.VMEM((2 * rows, hidden), F32),
            pltpu.VMEM((2 * rows, hidden), F32),
            pltpu.VMEM((2 * rows, hidden), BF16),
            pltpu.VMEM((2 * rows, toks), F32),
            pltpu.VMEM((ny, 2, rows, width), BF16),
            pltpu.VMEM((ny, rows, width), BF16),
            pltpu.VMEM((2, far, rows, width), BF16),
            pltpu.VMEM((2, rows, width), BF16),
            pltpu.VMEM((2, far, rows, width), BF16),
            pltpu.VMEM((rows, width), BF16),
            pltpu.VMEM((rows, width), BF16),
            dma((9,)),
            dma((2, 4, ne)),
            dma((2, 4, ne)),
            dma((2, 2, far - 2, 4)),
            dma((2, 2, far - 2, 4)),
            dma((2, ny)),
            dma((2, ny)),
            dma((ny,)),
            dma((ny,)),
            dma((2, far, 4)),
            dma((2, far, 4)),
            dma((ne,)),
            dma((ne,)),
            dma((2, 2, 4)),
            dma((2, 2, 4)),
            dma((2, 4)),
            dma((2, 4)),
            pltpu.SemaphoreType.REGULAR,
        ],
        compiler_params=pltpu.CompilerParams(
            collective_id=0, has_side_effects=True, vmem_limit_bytes=60 * 1024 * 1024
        ),
    )(tokens, routes.T, route_weights.T, w_gate, w_up, w_down)


def solution(mesh):
    return jax.shard_map(
        on_device,
        mesh=mesh,
        in_specs=(
            P(("dp", "expert"), None),
            P(("dp", "expert"), None),
            P(("dp", "expert"), None),
            P("expert", None, "pipe"),
            P("expert", None, "pipe"),
            P("expert", "pipe", None),
        ),
        out_specs=P(("dp", "expert"), "pipe"),
        check_vma=False,
    )
```

```python
import functools

import jax
import jax.numpy as jnp
from jax import lax
from jax.experimental import pallas as pl
from jax.experimental.pallas import tpu as pltpu
from jax.sharding import PartitionSpec as P

MESH = pl.DeviceIdType.MESH
F32 = jnp.float32
BF16 = jnp.bfloat16


def kernel(
    dims,
    tokens,
    routes,
    route_w,
    wg,
    wu,
    wd,
    out,
    route_v,
    weight_v,
    tok_v,
    xs,
    xbuf,
    wg_v,
    wu_v,
    wd_v,
    acc_g,
    acc_u,
    hid,
    mix,
    pk,
    cin,
    rin,
    rout,
    fin,
    rbuf,
    load_sem,
    xs_sem,
    xr_sem,
    ys_sem,
    yr_sem,
    cs_sem,
    cr_sem,
    ds_sem,
    dr_sem,
    rs_sem,
    rr_sem,
    fs_sem,
    fr_sem,
    ready,
):
    ne, ny, half, width = dims
    rows = ne * half
    parts = 4
    sub = rows // parts
    pipe = lax.axis_index("pipe")
    e = lax.axis_index("expert")
    y = pipe // 2
    c = pipe % 2
    d = lax.axis_index("dp")
    far = ny // 2
    hop = far - 1
    steps = far - 2

    def zero(v, n):
        return 1 - (v + n - 1) // n

    def carrier(at_y, at_e, h):
        if h == 1:
            return 1
        return zero(d, lax.axis_size("dp")) * zero(at_y, ny) * zero(at_e, ne)

    def chip(at_y, h):
        at_y = (at_y + ny) % ny
        return {"pipe": 2 * at_y + carrier(at_y, e, h)}

    def across(t, h):
        return {"pipe": 2 * y + carrier(y, t, h), "expert": t}

    right = {"pipe": (y + 1) % ny * 2 + c}
    left = {"pipe": (y + ny - 1) % ny * 2 + c}
    peer = {"pipe": 2 * y + 1 - c}
    front = d == 0
    lone = jnp.logical_and(front, jnp.logical_and(pipe == 0, e == 0))
    double = jnp.logical_and(front, jnp.logical_and(pipe == 1, e == 0))
    in_row = jnp.logical_and(y == 0, e != 0)
    in_column = jnp.logical_and(e == 0, jnp.logical_or(y == 1, y == ny - 1))
    beside = jnp.logical_and(jnp.logical_and(front, c == 0), jnp.logical_or(in_row, in_column))
    active = [carrier(y, e, h) == c for h in range(2)]

    def chunk(j):
        return (y + j + ny) % ny

    def at16(x):
        return pl.multiple_of(x, 16)

    def remote(src, dst, send, recv, device):
        return pltpu.make_async_remote_copy(
            src_ref=src, dst_ref=dst, send_sem=send, recv_sem=recv, device_id=device, device_id_type=MESH
        )

    sent = []
    sent_of = [[], []]

    def go(copy):
        copy.start()
        sent.append(copy)

    def send(h, make):
        make().start()
        sent_of[h].append(make)

    def carry(work):
        for h in range(2):

            @pl.when(active[h])
            def _():
                work(h)

    pairs = [(routes, route_v), (route_w, weight_v)]
    direct = [0, far] + [j for k in range(steps + 1, far) for j in (-k, k)]
    for i, j in enumerate(direct):
        cols = pl.ds(pl.multiple_of(chunk(j) * width, 128), width)
        pairs.append((tokens.at[:, cols], tok_v.at[i]))
    pairs += [(wg.at[0], wg_v), (wu.at[0], wu_v), (wd.at[0], wd_v)]
    loads = [pltpu.make_async_copy(src, dst, load_sem.at[i]) for i, (src, dst) in enumerate(pairs)]
    for copy in loads:
        copy.start()

    barrier = pltpu.get_barrier_semaphore()

    def greet(semaphore, device):
        pl.semaphore_signal(semaphore, inc=1, device_id=device, device_id_type=MESH)

    neighbours = [{"expert": (e + j) % ne} for j in range(1, ne)] + [right, left, peer]

    @pl.when(jnp.logical_not(lone))
    def _():
        for device in neighbours:
            greet(barrier, device)

    @pl.when(double)
    def _():
        for device in [{"pipe": 0, "expert": t} for t in range(1, ne)] + [{"pipe": 2}, {"pipe": 2 * ny - 2}]:
            greet(barrier, device)

    @pl.when(beside)
    def _():
        greet(barrier, {"pipe": 1, "expert": 0})

    toks = tok_v.shape[1]
    row = lax.broadcasted_iota(jnp.int32, (2 * rows, toks), 0)
    hbits, rbits = half.bit_length() - 1, rows.bit_length() - 1
    expert_of = (row >> hbits) & (ne - 1)
    slot_of = ((row >> rbits) << hbits) + (row & (half - 1))
    loads[0].wait()
    loads[1].wait()
    first = route_v[0:1, :] == expert_of
    second = route_v[1:2, :] == expert_of
    named = jnp.logical_or(first, second)
    before = (
        lax.broadcasted_iota(jnp.int32, (toks, toks), 0) < lax.broadcasted_iota(jnp.int32, (toks, toks), 1)
    ).astype(F32)
    rank = jnp.dot(named.astype(F32).astype(BF16), before.astype(BF16), preferred_element_type=F32)
    taken = jnp.logical_and(named, rank == slot_of.astype(F32))
    mix[...] = jnp.where(taken, jnp.where(first, weight_v[0:1, :], weight_v[1:2, :]), 0.0)
    picked = taken.astype(F32)
    picked = picked.astype(BF16)
    loads[2].wait()
    xs[0] = jnp.dot(picked, tok_v[0], preferred_element_type=F32).astype(BF16)

    @pl.when(jnp.logical_not(double))
    def _():
        pl.semaphore_wait(barrier, len(neighbours))

    @pl.when(double)
    def _():
        pl.semaphore_wait(barrier, 2 * len(neighbours) - 2)

    @pl.when(lone)
    def _():
        for device in neighbours:
            greet(ready, device)

    far_first = sorted(range(1, ne), key=lambda n: -min(n, ne - n))

    def slab(core, t):
        return pl.ds(at16(core * rows + t * half), half)

    def x_copy(h, i, n):
        t = (e + n) % ne
        return remote(
            xs.at[i, slab(h, t)],
            xbuf.at[chunk(direct[i]), slab(h, e)],
            xs_sem.at[h, i, n],
            xr_sem.at[h, i, n],
            across(t, h),
        )

    def x_send(h, i):
        for n in far_first:
            send(h, functools.partial(x_copy, h, i, n))
        xbuf[chunk(direct[i]), slab(h, e), :] = xs[i, slab(h, e), :]

    def x_arrived(h, i):
        for n in reversed(far_first):
            t = (e + ne - n) % ne
            remote(
                xs.at[i, slab(h, 0)],
                xbuf.at[chunk(direct[i]), slab(h, t)],
                xs_sem.at[h, i, n],
                xr_sem.at[h, i, n],
                across(t, h),
            ).wait_recv()

    def y_copy(h, way, s, b, arriving=False):
        j = s + 1 if arriving else s
        ref = xbuf.at[chunk(-j if way == 0 else j), pl.ds(h * rows + b * sub, sub)]
        return remote(
            ref, ref, ys_sem.at[h, way, s, b], yr_sem.at[h, way, s, b], chip(y + 1 if way == 0 else y - 1, h)
        )

    def share_copy(h, j):
        ref = xbuf.at[chunk(j), pl.ds(h * rows, rows)]
        return remote(ref, ref, cs_sem.at[h, j + hop], cr_sem.at[h, j + hop], peer)

    def share(h, *chunks):
        for j in chunks:
            send(h, functools.partial(share_copy, h, j))

    def gemm(j, start=False):
        k = chunk(j)
        for h in range(2):

            @pl.when(jnp.logical_not(active[h]))
            def _():
                share_copy(h, j).wait_recv()

        lhs = xbuf[k]
        deep = pl.ds(pl.multiple_of(k * width, 128), width)
        for acc, w in ((acc_g, wg_v), (acc_u, wu_v)):
            term = jnp.dot(lhs, w[deep, :], preferred_element_type=F32)
            acc[...] = term if start else acc[...] + term

    carry(lambda h: x_send(h, 0))
    for i in range(1, len(direct)):
        loads[2 + i].wait()
        xs[i] = jnp.dot(picked, tok_v[i], preferred_element_type=F32).astype(BF16)
        carry(lambda h: x_send(h, i))

    def first_hop(h):
        x_arrived(h, 0)
        for b in range(parts):
            for way in range(2):
                send(h, functools.partial(y_copy, h, way, 0, b))

    def next_hop(s, h):
        for b in range(parts):
            for way in range(2):
                y_copy(h, way, s, b, True).wait_recv()
                if s + 1 < steps:
                    send(h, functools.partial(y_copy, h, way, s + 1, b))

    def x_rest(h, i):
        x_arrived(h, i)
        share(h, direct[i])

    def last_hop(h):
        next_hop(steps - 1, h)
        share(h, -steps, steps)

    carry(first_hop)

    @pl.when(jnp.logical_not(jnp.logical_or(double, lone)))
    def _():
        for h in range(2):

            @pl.when(active[h])
            def _():
                share_copy(h, 0).start()

    for s in range(steps - 1):
        carry(functools.partial(next_hop, s))

    @pl.when(double)
    def _():
        pl.semaphore_wait(ready, 1)
        share_copy(0, 0).start()
        share_copy(1, 0).start()

    for h in range(2):
        sent_of[h].append(functools.partial(share_copy, h, 0))
    carry(lambda h: share(h, *[j for k in range(1, steps) for j in (-k, k)]))
    ahead = len(pairs) - 3
    loads[ahead].wait()
    loads[ahead + 1].wait()
    gemm(0, True)
    carry(lambda h: x_rest(h, 1))
    for k in range(1, steps):
        gemm(-k)
        gemm(k)
    carry(lambda h: x_rest(h, 2))
    gemm(far)
    carry(last_hop)
    for i in range(3, len(direct)):
        carry(lambda h: x_rest(h, i))
    for j in (direct[2], -steps, steps, *direct[3:]):
        gemm(j)

    @pl.when(beside)
    def _():
        pl.semaphore_wait(ready, 1)

    gate = acc_g[...]
    hid[...] = (gate / (1.0 + jnp.exp(-gate)) * acc_u[...]).astype(BF16)
    loads[ahead + 2].wait()

    low = lax.broadcasted_iota(jnp.int32, (rows, width), 1) < width // 2

    def down(j):
        i = j + hop
        cols = pl.ds(pl.multiple_of(chunk(j) * width, 128), width)
        part = jnp.dot(hid[...], wd_v[:, cols], preferred_element_type=F32)
        a, b = part[:rows], part[rows:]
        pk[i, 0] = jnp.where(low, a, pltpu.roll(b, width // 2, 1)).astype(BF16)
        pk[i, 1] = jnp.where(low, pltpu.roll(a, width // 2, 1), b).astype(BF16)
        go(remote(pk.at[i, 1 - c], cin.at[i], ds_sem.at[i], dr_sem.at[i], peer))

    def met(j):
        i = j + hop
        remote(pk.at[i, 1 - c], cin.at[i], ds_sem.at[i], dr_sem.at[i], peer).wait_recv()

    def own(j, b):
        i = j + hop
        at = pl.ds(b * sub, sub)
        return pk[i, c, at, :].astype(F32) + cin[i, at, :].astype(F32)

    def r_copy(way, s, b):
        at = pl.ds(b * sub, sub)
        return remote(
            rout.at[way, s, at],
            rin.at[way, s, at],
            rs_sem.at[way, s, b],
            rr_sem.at[way, s, b],
            right if way == 0 else left,
        )

    def got(way, s, b):
        r_copy(way, s, b).wait_recv()
        return rin[way, s, pl.ds(b * sub, sub), :].astype(F32)

    def pass_on(way, s, b):
        if s == 0:
            total = own(far, b)
        else:
            total = own(far - s if way == 0 else s - far, b)
            if s > 1 or b // (parts // 2) == way:
                total = total + got(way, s - 1, b)
        rout[way, s, pl.ds(b * sub, sub), :] = total.astype(BF16)
        go(r_copy(way, s, b))

    down(far)
    for j in range(far - 1, max(0, far - 3), -1):
        down(j)
        down(-j)
    early, late = range(parts // 2), range(parts // 2, parts)
    met(far)
    for b in early:
        pass_on(0, 0, b)
        pass_on(1, 0, parts - 1 - b)
    met(far - 1)
    met(1 - far)
    for b in late:
        pass_on(0, 1, b)
        pass_on(1, 1, parts - 1 - b)
    for j in range(far - 3, 0, -1):
        down(j)
        down(-j)
    down(0)
    for b in early:
        pass_on(0, 1, b)
        pass_on(1, 1, parts - 1 - b)
    for s in range(2, far):
        met(far - s)
        met(s - far)
        for b in (*late, *early):
            pass_on(0, s, b)
            pass_on(1, s, parts - 1 - b)
    met(0)

    per = ne // parts
    own_back = pl.ds(at16(e * half), half)

    def back_copy(t):
        return remote(
            fin.at[pl.ds(t * half, half)], rbuf.at[own_back], fs_sem.at[t], fr_sem.at[e], {"expert": t}
        )

    order = [b for pair in zip(late, reversed(early)) for b in pair]
    for b in order:
        total = own(0, b) + got(0, far - 1, b) + got(1, far - 1, b)
        fin[pl.ds(b * sub, sub), :] = total.astype(BF16)
        for t in range(b * per, b * per + per):

            @pl.when(t != e)
            def _():
                back_copy(t).start()

    rbuf[own_back, :] = fin[own_back, :]
    weights = mix[...].T
    hi = weights.astype(BF16)
    lo = (weights - hi.astype(F32)).astype(BF16)
    for copy in sent:
        copy.wait_send()
    carry(lambda h: [make().wait_send() for make in sent_of[h]])
    for n in range(1, ne):
        t = (e + n) % ne
        at = pl.ds(at16(t * half), half)
        remote(fin.at[at], rbuf.at[at], fs_sem.at[t], fr_sem.at[t], {"expert": t}).wait()
    back = rbuf[...]

    def mixed(side):
        cols = slice(side * rows, side * rows + rows)
        return jnp.dot(hi[:, cols], back, preferred_element_type=F32) + jnp.dot(
            lo[:, cols], back, preferred_element_type=F32
        )

    total = mixed(0) + pltpu.roll(mixed(1), width // 2, 1)
    out[...] = total[:, : width // 2].astype(BF16)


def on_device(tokens, routes, route_weights, w_gate, w_up, w_down):
    ne = lax.axis_size("expert")
    ny = lax.axis_size("pipe") // 2
    toks, model = tokens.shape
    hidden = w_gate.shape[2]
    width = model // ny
    half = 16
    rows = ne * half
    far = ny // 2
    vmem = pl.BlockSpec(memory_space=pltpu.VMEM)
    hbm = pl.BlockSpec(memory_space=pl.ANY)
    dma = pltpu.SemaphoreType.DMA
    return pl.pallas_call(
        functools.partial(kernel, (ne, ny, half, width)),
        out_shape=jax.ShapeDtypeStruct((toks, width // 2), BF16),
        in_specs=[hbm] * 6,
        out_specs=vmem,
        scratch_shapes=[
            pltpu.VMEM((2, toks), jnp.int32),
            pltpu.VMEM((2, toks), F32),
            pltpu.VMEM((4, toks, width), BF16),
            pltpu.VMEM((4, 2 * rows, width), BF16),
            pltpu.VMEM((ny, 2 * rows, width), BF16),
            pltpu.VMEM((model, hidden), BF16),
            pltpu.VMEM((model, hidden), BF16),
            pltpu.VMEM((hidden, model), BF16),
            pltpu.VMEM((2 * rows, hidden), F32),
            pltpu.VMEM((2 * rows, hidden), F32),
            pltpu.VMEM((2 * rows, hidden), BF16),
            pltpu.VMEM((2 * rows, toks), F32),
            pltpu.VMEM((ny, 2, rows, width), BF16),
            pltpu.VMEM((ny, rows, width), BF16),
            pltpu.VMEM((2, far, rows, width), BF16),
            pltpu.VMEM((2, far, rows, width), BF16),
            pltpu.VMEM((rows, width), BF16),
            pltpu.VMEM((rows, width), BF16),
            dma((9,)),
            dma((2, 4, ne)),
            dma((2, 4, ne)),
            dma((2, 2, far - 2, 4)),
            dma((2, 2, far - 2, 4)),
            dma((2, ny)),
            dma((2, ny)),
            dma((ny,)),
            dma((ny,)),
            dma((2, far, 4)),
            dma((2, far, 4)),
            dma((ne,)),
            dma((ne,)),
            pltpu.SemaphoreType.REGULAR,
        ],
        compiler_params=pltpu.CompilerParams(
            collective_id=0, has_side_effects=True, vmem_limit_bytes=54784 * 1024
        ),
    )(tokens, routes.T, route_weights.T, w_gate, w_up, w_down)


def solution(mesh):
    return jax.shard_map(
        on_device,
        mesh=mesh,
        in_specs=(
            P(("dp", "expert"), None),
            P(("dp", "expert"), None),
            P(("dp", "expert"), None),
            P("expert", None, "pipe"),
            P("expert", None, "pipe"),
            P("expert", "pipe", None),
        ),
        out_specs=P(("dp", "expert"), "pipe"),
        check_vma=False,
    )
```

```python
import functools

import jax
import jax.numpy as jnp
from jax import lax
from jax.experimental import pallas as pl
from jax.experimental.pallas import tpu as pltpu
from jax.sharding import PartitionSpec as P

MESH = pl.DeviceIdType.MESH
F32 = jnp.float32
BF16 = jnp.bfloat16


def kernel(
    dims,
    tokens,
    routes,
    route_w,
    wg,
    wu,
    wd,
    out,
    route_v,
    weight_v,
    tok_v,
    xs,
    xbuf,
    wg_v,
    wu_v,
    wd_v,
    acc_g,
    acc_u,
    hid,
    mix,
    pk,
    cin,
    rin,
    rout,
    fin,
    rbuf,
    load_sem,
    xs_sem,
    xr_sem,
    ys_sem,
    yr_sem,
    cs_sem,
    cr_sem,
    ds_sem,
    dr_sem,
    rs_sem,
    rr_sem,
    fs_sem,
    fr_sem,
    ready,
):
    ne, ny, half, width = dims
    rows = ne * half
    parts = 4
    sub = rows // parts
    per = ne // parts
    pipe = lax.axis_index("pipe")
    e = lax.axis_index("expert")
    y = pipe // 2
    c = pipe % 2
    d = lax.axis_index("dp")
    far = ny // 2
    hop = far - 1
    steps = far - 2

    def zero(v, n):
        return 1 - (v + n - 1) // n

    def carrier(at_y, at_e, h):
        if h == 1:
            return 1
        return zero(d, lax.axis_size("dp")) * zero(at_y, ny) * zero(at_e, ne)

    def chip(at_y, h):
        at_y = (at_y + ny) % ny
        return {"pipe": 2 * at_y + carrier(at_y, e, h)}

    def across(t, h):
        return {"pipe": 2 * y + carrier(y, t, h), "expert": t}

    right = {"pipe": (y + 1) % ny * 2 + c}
    left = {"pipe": (y + ny - 1) % ny * 2 + c}
    peer = {"pipe": 2 * y + 1 - c}
    front = d == 0
    lone = jnp.logical_and(front, jnp.logical_and(pipe == 0, e == 0))
    double = jnp.logical_and(front, jnp.logical_and(pipe == 1, e == 0))
    in_row = jnp.logical_and(y == 0, e != 0)
    in_column = jnp.logical_and(e == 0, jnp.logical_or(y == 1, y == ny - 1))
    beside = jnp.logical_and(jnp.logical_and(front, c == 0), jnp.logical_or(in_row, in_column))
    active = [carrier(y, e, h) == c for h in range(2)]

    def chunk(j):
        return (y + j + ny) % ny

    base = e // per
    near_first, far_first_parts = (0, 1, 3, 2), (2, 1, 3, 0)

    def part(k):
        return pl.multiple_of((base + k) % parts * sub, sub)

    def others(k):
        if k:
            return [(base + k) % parts * per + m for m in range(per)]
        return [base * per + (e + m) % per for m in range(1, per)]

    def at16(x):
        return pl.multiple_of(x, 16)

    def remote(src, dst, send, recv, device):
        return pltpu.make_async_remote_copy(
            src_ref=src, dst_ref=dst, send_sem=send, recv_sem=recv, device_id=device, device_id_type=MESH
        )

    sent = []
    sent_of = [[], []]

    def go(copy):
        copy.start()
        sent.append(copy)

    def send(h, make):
        make().start()
        sent_of[h].append(make)

    def carry(work):
        for h in range(2):

            @pl.when(active[h])
            def _():
                work(h)

    pairs = [(routes, route_v), (route_w, weight_v)]
    direct = [0, far] + [j for k in range(steps + 1, far) for j in (-k, k)]
    for i, j in enumerate(direct):
        cols = pl.ds(pl.multiple_of(chunk(j) * width, 128), width)
        pairs.append((tokens.at[:, cols], tok_v.at[i]))
    pairs += [(wg.at[0], wg_v), (wu.at[0], wu_v), (wd.at[0], wd_v)]
    loads = [pltpu.make_async_copy(src, dst, load_sem.at[i]) for i, (src, dst) in enumerate(pairs)]
    for copy in loads:
        copy.start()

    barrier = pltpu.get_barrier_semaphore()

    def greet(semaphore, device):
        pl.semaphore_signal(semaphore, inc=1, device_id=device, device_id_type=MESH)

    neighbours = [{"expert": (e + j) % ne} for j in range(1, ne)] + [right, left, peer]

    @pl.when(jnp.logical_not(lone))
    def _():
        for device in neighbours:
            greet(barrier, device)

    @pl.when(double)
    def _():
        for device in [{"pipe": 0, "expert": t} for t in range(1, ne)] + [{"pipe": 2}, {"pipe": 2 * ny - 2}]:
            greet(barrier, device)

    @pl.when(beside)
    def _():
        greet(barrier, {"pipe": 1, "expert": 0})

    toks = tok_v.shape[1]
    row = lax.broadcasted_iota(jnp.int32, (2 * rows, toks), 0)
    hbits, rbits = half.bit_length() - 1, rows.bit_length() - 1
    expert_of = (row >> hbits) & (ne - 1)
    slot_of = ((row >> rbits) << hbits) + (row & (half - 1))
    loads[0].wait()
    loads[1].wait()
    first = route_v[0:1, :] == expert_of
    second = route_v[1:2, :] == expert_of
    named = jnp.logical_or(first, second)
    before = (
        lax.broadcasted_iota(jnp.int32, (toks, toks), 0) < lax.broadcasted_iota(jnp.int32, (toks, toks), 1)
    ).astype(F32)
    rank = jnp.dot(named.astype(F32).astype(BF16), before.astype(BF16), preferred_element_type=F32)
    taken = jnp.logical_and(named, rank == slot_of.astype(F32))
    mix[...] = jnp.where(taken, jnp.where(first, weight_v[0:1, :], weight_v[1:2, :]), 0.0)
    picked = taken.astype(F32)
    picked = picked.astype(BF16)
    loads[2].wait()
    xs[0] = jnp.dot(picked, tok_v[0], preferred_element_type=F32).astype(BF16)

    @pl.when(jnp.logical_not(double))
    def _():
        pl.semaphore_wait(barrier, len(neighbours))

    @pl.when(double)
    def _():
        pl.semaphore_wait(barrier, 2 * len(neighbours) - 2)

    @pl.when(lone)
    def _():
        for device in neighbours:
            greet(ready, device)

    far_first = sorted(range(1, ne), key=lambda n: -min(n, ne - n))

    def slab(core, t):
        return pl.ds(at16(core * rows + t * half), half)

    def x_copy(h, i, n):
        t = (e + n) % ne
        return remote(
            xs.at[i, slab(h, t)],
            xbuf.at[chunk(direct[i]), slab(h, e)],
            xs_sem.at[h, i, n],
            xr_sem.at[h, i, n],
            across(t, h),
        )

    def x_send(h, i):
        for n in far_first:
            send(h, functools.partial(x_copy, h, i, n))
        xbuf[chunk(direct[i]), slab(h, e), :] = xs[i, slab(h, e), :]

    def x_arrived(h, i):
        for n in reversed(far_first):
            t = (e + ne - n) % ne
            remote(
                xs.at[i, slab(h, 0)],
                xbuf.at[chunk(direct[i]), slab(h, t)],
                xs_sem.at[h, i, n],
                xr_sem.at[h, i, n],
                across(t, h),
            ).wait_recv()

    def y_copy(h, way, s, b, arriving=False):
        j = s + 1 if arriving else s
        ref = xbuf.at[chunk(-j if way == 0 else j), pl.ds(pl.multiple_of(h * rows + part(b), sub), sub)]
        return remote(
            ref, ref, ys_sem.at[h, way, s, b], yr_sem.at[h, way, s, b], chip(y + 1 if way == 0 else y - 1, h)
        )

    def share_copy(h, j):
        ref = xbuf.at[chunk(j), pl.ds(h * rows, rows)]
        return remote(ref, ref, cs_sem.at[h, j + hop], cr_sem.at[h, j + hop], peer)

    def share(h, *chunks):
        for j in chunks:
            send(h, functools.partial(share_copy, h, j))

    def gemm(j, start=False):
        k = chunk(j)
        for h in range(2):

            @pl.when(jnp.logical_not(active[h]))
            def _():
                share_copy(h, j).wait_recv()

        lhs = xbuf[k]
        deep = pl.ds(pl.multiple_of(k * width, 128), width)
        for acc, w in ((acc_g, wg_v), (acc_u, wu_v)):
            term = jnp.dot(lhs, w[deep, :], preferred_element_type=F32)
            acc[...] = term if start else acc[...] + term

    carry(lambda h: x_send(h, 0))
    for i in range(1, len(direct)):
        loads[2 + i].wait()
        xs[i] = jnp.dot(picked, tok_v[i], preferred_element_type=F32).astype(BF16)
        carry(lambda h: x_send(h, i))

    def first_hop(h):
        for b in near_first:
            for t in others(b):
                n = (e + ne - t) % ne
                remote(
                    xs.at[0, slab(h, 0)],
                    xbuf.at[chunk(0), slab(h, t)],
                    xs_sem.at[h, 0, n],
                    xr_sem.at[h, 0, n],
                    across(t, h),
                ).wait_recv()
            for way in range(2):
                send(h, functools.partial(y_copy, h, way, 0, b))

    def next_hop(s, h):
        for b in near_first:
            for way in range(2):
                y_copy(h, way, s, b, True).wait_recv()
                if s + 1 < steps:
                    send(h, functools.partial(y_copy, h, way, s + 1, b))

    def x_rest(h, i):
        x_arrived(h, i)
        share(h, direct[i])

    def last_hop(h):
        next_hop(steps - 1, h)
        share(h, -steps, steps)

    carry(first_hop)

    @pl.when(jnp.logical_not(jnp.logical_or(double, lone)))
    def _():
        for h in range(2):

            @pl.when(active[h])
            def _():
                share_copy(h, 0).start()

    for s in range(steps - 1):
        carry(functools.partial(next_hop, s))

    @pl.when(double)
    def _():
        pl.semaphore_wait(ready, 1)
        share_copy(0, 0).start()
        share_copy(1, 0).start()

    for h in range(2):
        sent_of[h].append(functools.partial(share_copy, h, 0))
    carry(lambda h: share(h, *[j for k in range(1, steps) for j in (-k, k)]))
    ahead = len(pairs) - 3
    loads[ahead].wait()
    loads[ahead + 1].wait()
    gemm(0, True)
    carry(lambda h: x_rest(h, 1))
    for k in range(1, steps):
        gemm(-k)
        gemm(k)
    carry(lambda h: x_rest(h, 2))
    gemm(far)
    carry(last_hop)
    for i in range(3, len(direct)):
        carry(lambda h: x_rest(h, i))
    for j in (direct[2], -steps, steps, *direct[3:]):
        gemm(j)

    @pl.when(beside)
    def _():
        pl.semaphore_wait(ready, 1)

    gate = acc_g[...]
    hid[...] = (gate / (1.0 + jnp.exp(-gate)) * acc_u[...]).astype(BF16)
    loads[ahead + 2].wait()

    low = lax.broadcasted_iota(jnp.int32, (rows, width), 1) < width // 2

    def down(j):
        i = j + hop
        cols = pl.ds(pl.multiple_of(chunk(j) * width, 128), width)
        part = jnp.dot(hid[...], wd_v[:, cols], preferred_element_type=F32)
        a, b = part[:rows], part[rows:]
        pk[i, 0] = jnp.where(low, a, pltpu.roll(b, width // 2, 1)).astype(BF16)
        pk[i, 1] = jnp.where(low, pltpu.roll(a, width // 2, 1), b).astype(BF16)
        go(remote(pk.at[i, 1 - c], cin.at[i], ds_sem.at[i], dr_sem.at[i], peer))

    def met(j):
        i = j + hop
        remote(pk.at[i, 1 - c], cin.at[i], ds_sem.at[i], dr_sem.at[i], peer).wait_recv()

    def own(j, b):
        i = j + hop
        at = pl.ds(part(b), sub)
        return pk[i, c, at, :].astype(F32) + cin[i, at, :].astype(F32)

    def r_copy(way, s, b):
        at = pl.ds(part(b), sub)
        return remote(
            rout.at[way, s, at],
            rin.at[way, s, at],
            rs_sem.at[way, s, b],
            rr_sem.at[way, s, b],
            right if way == 0 else left,
        )

    def got(way, s, b):
        r_copy(way, s, b).wait_recv()
        return rin[way, s, pl.ds(part(b), sub), :].astype(F32)

    def pass_on(way, s, b):
        if s == 0:
            total = own(far, b)
        else:
            total = own(far - s if way == 0 else s - far, b)
            if s > 1 or b // (parts // 2) == way:
                total = total + got(way, s - 1, b)
        rout[way, s, pl.ds(part(b), sub), :] = total.astype(BF16)
        go(r_copy(way, s, b))

    down(far)
    for j in range(far - 1, max(0, far - 3), -1):
        down(j)
        down(-j)
    early, late = (1, 0), (2, 3)
    met(far)
    for b in early:
        pass_on(0, 0, b)
        pass_on(1, 0, parts - 1 - b)
    met(far - 1)
    met(1 - far)
    for b in late:
        pass_on(0, 1, b)
        pass_on(1, 1, parts - 1 - b)
    for j in range(far - 3, 0, -1):
        down(j)
        down(-j)
    down(0)
    for b in early:
        pass_on(0, 1, b)
        pass_on(1, 1, parts - 1 - b)
    for s in range(2, far):
        met(far - s)
        met(s - far)
        for b in far_first_parts:
            pass_on(0, s, b)
            pass_on(1, s, b)
    met(0)

    own_back = pl.ds(at16(e * half), half)

    def back_copy(t):
        return remote(
            fin.at[pl.ds(at16(t * half), half)], rbuf.at[own_back], fs_sem.at[t], fr_sem.at[e], {"expert": t}
        )

    for b in far_first_parts:
        total = own(0, b) + got(0, far - 1, b) + got(1, far - 1, b)
        fin[pl.ds(part(b), sub), :] = total.astype(BF16)
        for t in others(b):
            back_copy(t).start()

    rbuf[own_back, :] = fin[own_back, :]
    weights = mix[...].T
    hi = weights.astype(BF16)
    lo = (weights - hi.astype(F32)).astype(BF16)
    for copy in sent:
        copy.wait_send()
    carry(lambda h: [make().wait_send() for make in sent_of[h]])
    for n in range(1, ne):
        t = (e + n) % ne
        at = pl.ds(at16(t * half), half)
        remote(fin.at[at], rbuf.at[at], fs_sem.at[t], fr_sem.at[t], {"expert": t}).wait()
    back = rbuf[...]

    def mixed(side):
        cols = slice(side * rows, side * rows + rows)
        return jnp.dot(hi[:, cols], back, preferred_element_type=F32) + jnp.dot(
            lo[:, cols], back, preferred_element_type=F32
        )

    total = mixed(0) + pltpu.roll(mixed(1), width // 2, 1)
    out[...] = total[:, : width // 2].astype(BF16)


def on_device(tokens, routes, route_weights, w_gate, w_up, w_down):
    ne = lax.axis_size("expert")
    ny = lax.axis_size("pipe") // 2
    toks, model = tokens.shape
    hidden = w_gate.shape[2]
    width = model // ny
    half = 16
    rows = ne * half
    far = ny // 2
    vmem = pl.BlockSpec(memory_space=pltpu.VMEM)
    hbm = pl.BlockSpec(memory_space=pl.ANY)
    dma = pltpu.SemaphoreType.DMA
    return pl.pallas_call(
        functools.partial(kernel, (ne, ny, half, width)),
        out_shape=jax.ShapeDtypeStruct((toks, width // 2), BF16),
        in_specs=[hbm] * 6,
        out_specs=vmem,
        scratch_shapes=[
            pltpu.VMEM((2, toks), jnp.int32),
            pltpu.VMEM((2, toks), F32),
            pltpu.VMEM((4, toks, width), BF16),
            pltpu.VMEM((4, 2 * rows, width), BF16),
            pltpu.VMEM((ny, 2 * rows, width), BF16),
            pltpu.VMEM((model, hidden), BF16),
            pltpu.VMEM((model, hidden), BF16),
            pltpu.VMEM((hidden, model), BF16),
            pltpu.VMEM((2 * rows, hidden), F32),
            pltpu.VMEM((2 * rows, hidden), F32),
            pltpu.VMEM((2 * rows, hidden), BF16),
            pltpu.VMEM((2 * rows, toks), F32),
            pltpu.VMEM((ny, 2, rows, width), BF16),
            pltpu.VMEM((ny, rows, width), BF16),
            pltpu.VMEM((2, far, rows, width), BF16),
            pltpu.VMEM((2, far, rows, width), BF16),
            pltpu.VMEM((rows, width), BF16),
            pltpu.VMEM((rows, width), BF16),
            dma((9,)),
            dma((2, 4, ne)),
            dma((2, 4, ne)),
            dma((2, 2, far - 2, 4)),
            dma((2, 2, far - 2, 4)),
            dma((2, ny)),
            dma((2, ny)),
            dma((ny,)),
            dma((ny,)),
            dma((2, far, 4)),
            dma((2, far, 4)),
            dma((ne,)),
            dma((ne,)),
            pltpu.SemaphoreType.REGULAR,
        ],
        compiler_params=pltpu.CompilerParams(
            collective_id=0, has_side_effects=True, vmem_limit_bytes=54784 * 1024
        ),
    )(tokens, routes.T, route_weights.T, w_gate, w_up, w_down)


def solution(mesh):
    return jax.shard_map(
        on_device,
        mesh=mesh,
        in_specs=(
            P(("dp", "expert"), None),
            P(("dp", "expert"), None),
            P(("dp", "expert"), None),
            P("expert", None, "pipe"),
            P("expert", None, "pipe"),
            P("expert", "pipe", None),
        ),
        out_specs=P(("dp", "expert"), "pipe"),
        check_vma=False,
    )
```

```python
import functools

import jax
import jax.numpy as jnp
from jax import lax
from jax.experimental import pallas as pl
from jax.experimental.pallas import tpu as pltpu
from jax.sharding import PartitionSpec as P

MESH = pl.DeviceIdType.MESH
F32 = jnp.float32
BF16 = jnp.bfloat16


def kernel(
    dims,
    tokens,
    routes,
    route_w,
    wg,
    wu,
    wd,
    out,
    route_v,
    weight_v,
    tok_v,
    xs,
    xbuf,
    wg_v,
    wu_v,
    wd_v,
    acc_g,
    acc_u,
    hid,
    mix,
    pk,
    cin,
    rin,
    rout,
    fin,
    rbuf,
    load_sem,
    xs_sem,
    xr_sem,
    ys_sem,
    yr_sem,
    cs_sem,
    cr_sem,
    ds_sem,
    dr_sem,
    rs_sem,
    rr_sem,
    fs_sem,
    fr_sem,
    ready,
):
    ne, ny, half, width = dims
    rows = ne * half
    parts = 4
    sub = rows // parts
    per = ne // parts
    pipe = lax.axis_index("pipe")
    e = lax.axis_index("expert")
    y = pipe // 2
    c = pipe % 2
    d = lax.axis_index("dp")
    far = ny // 2
    hop = far - 1
    steps = far - 2

    def zero(v, n):
        return 1 - (v + n - 1) // n

    def carrier(at_y, at_e, h):
        if h == 1:
            return 1
        return zero(d, lax.axis_size("dp")) * zero(at_y, ny) * zero(at_e, ne)

    def chip(at_y, h):
        at_y = (at_y + ny) % ny
        return {"pipe": 2 * at_y + carrier(at_y, e, h)}

    def across(t, h):
        return {"pipe": 2 * y + carrier(y, t, h), "expert": t}

    right = {"pipe": (y + 1) % ny * 2 + c}
    left = {"pipe": (y + ny - 1) % ny * 2 + c}
    peer = {"pipe": 2 * y + 1 - c}
    two_on = [{"pipe": (y + 2) % ny * 2 + c}, {"pipe": (y + ny - 2) % ny * 2 + c}]
    front = d == 0
    lone = jnp.logical_and(front, jnp.logical_and(pipe == 0, e == 0))
    double = jnp.logical_and(front, jnp.logical_and(pipe == 1, e == 0))
    in_row = jnp.logical_and(y == 0, e != 0)
    in_column = jnp.logical_and(e == 0, jnp.logical_or(y == 1, y == ny - 1))
    in_second = jnp.logical_and(e == 0, jnp.logical_or(y == 2, y == ny - 2))
    second_on = jnp.logical_and(jnp.logical_and(front, c == 0), in_second)
    beside = jnp.logical_and(jnp.logical_and(front, c == 0), jnp.logical_or(in_row, in_column))
    active = [carrier(y, e, h) == c for h in range(2)]

    def chunk(j):
        return (y + j + ny) % ny

    base = e // per
    near_first, far_first_parts = (0, 1, 3, 2), (2, 1, 3, 0)

    def part(k):
        return pl.multiple_of((base + k) % parts * sub, sub)

    def others(k):
        if k:
            return [(base + k) % parts * per + m for m in range(per)]
        return [base * per + (e + m) % per for m in range(1, per)]

    def at16(x):
        return pl.multiple_of(x, 16)

    def remote(src, dst, send, recv, device):
        return pltpu.make_async_remote_copy(
            src_ref=src, dst_ref=dst, send_sem=send, recv_sem=recv, device_id=device, device_id_type=MESH
        )

    sent = []
    sent_of = [[], []]

    def go(copy):
        copy.start()
        sent.append(copy)

    def send(h, make):
        make().start()
        sent_of[h].append(make)

    def carry(work):
        for h in range(2):

            @pl.when(active[h])
            def _():
                work(h)

    pairs = [(routes, route_v), (route_w, weight_v)]
    direct = [0, far] + [j for k in range(steps + 1, far) for j in (-k, k)]
    for i, j in enumerate(direct):
        cols = pl.ds(pl.multiple_of(chunk(j) * width, 128), width)
        pairs.append((tokens.at[:, cols], tok_v.at[i]))
    pairs += [(wg.at[0], wg_v), (wu.at[0], wu_v), (wd.at[0], wd_v)]
    loads = [pltpu.make_async_copy(src, dst, load_sem.at[i]) for i, (src, dst) in enumerate(pairs)]
    for copy in loads:
        copy.start()

    barrier = pltpu.get_barrier_semaphore()

    def greet(semaphore, device):
        pl.semaphore_signal(semaphore, inc=1, device_id=device, device_id_type=MESH)

    neighbours = [{"expert": (e + j) % ne} for j in range(1, ne)] + [right, left, peer, *two_on]

    @pl.when(jnp.logical_not(lone))
    def _():
        for device in neighbours:
            greet(barrier, device)

    @pl.when(double)
    def _():
        for device in [{"pipe": 0, "expert": t} for t in range(1, ne)] + [{"pipe": 2}, {"pipe": 2 * ny - 2}]:
            greet(barrier, device)

    @pl.when(beside)
    def _():
        greet(barrier, {"pipe": 1, "expert": 0})

    toks = tok_v.shape[1]
    row = lax.broadcasted_iota(jnp.int32, (2 * rows, toks), 0)
    hbits, rbits = half.bit_length() - 1, rows.bit_length() - 1
    expert_of = (row >> hbits) & (ne - 1)
    slot_of = ((row >> rbits) << hbits) + (row & (half - 1))
    loads[0].wait()
    loads[1].wait()
    first = route_v[0:1, :] == expert_of
    second = route_v[1:2, :] == expert_of
    named = jnp.logical_or(first, second)
    before = (
        lax.broadcasted_iota(jnp.int32, (toks, toks), 0) < lax.broadcasted_iota(jnp.int32, (toks, toks), 1)
    ).astype(F32)
    rank = jnp.dot(named.astype(F32).astype(BF16), before.astype(BF16), preferred_element_type=F32)
    taken = jnp.logical_and(named, rank == slot_of.astype(F32))
    mix[...] = jnp.where(taken, jnp.where(first, weight_v[0:1, :], weight_v[1:2, :]), 0.0)
    picked = taken.astype(F32)
    picked = picked.astype(BF16)
    loads[2].wait()
    xs[0] = jnp.dot(picked, tok_v[0], preferred_element_type=F32).astype(BF16)

    @pl.when(jnp.logical_not(jnp.logical_or(double, second_on)))
    def _():
        pl.semaphore_wait(barrier, len(neighbours))

    @pl.when(second_on)
    def _():
        pl.semaphore_wait(barrier, len(neighbours) - 1)

    @pl.when(double)
    def _():
        pl.semaphore_wait(barrier, len(neighbours) - 1 + ne - 1 + 2)

    @pl.when(lone)
    def _():
        for device in neighbours:
            greet(ready, device)

    far_first = sorted(range(1, ne), key=lambda n: -min(n, ne - n))

    def slab(core, t):
        return pl.ds(at16(core * rows + t * half), half)

    def x_copy(h, i, n):
        t = (e + n) % ne
        return remote(
            xs.at[i, slab(h, t)],
            xbuf.at[chunk(direct[i]), slab(h, e)],
            xs_sem.at[h, i, n],
            xr_sem.at[h, i, n],
            across(t, h),
        )

    def x_send(h, i):
        for n in far_first:
            send(h, functools.partial(x_copy, h, i, n))
        xbuf[chunk(direct[i]), slab(h, e), :] = xs[i, slab(h, e), :]

    def x_arrived(h, i):
        for n in reversed(far_first):
            t = (e + ne - n) % ne
            remote(
                xs.at[i, slab(h, 0)],
                xbuf.at[chunk(direct[i]), slab(h, t)],
                xs_sem.at[h, i, n],
                xr_sem.at[h, i, n],
                across(t, h),
            ).wait_recv()

    def y_copy(h, way, s, b, arriving=False):
        j = s + 1 if arriving else s
        ref = xbuf.at[chunk(-j if way == 0 else j), pl.ds(pl.multiple_of(h * rows + part(b), sub), sub)]
        return remote(
            ref, ref, ys_sem.at[h, way, s, b], yr_sem.at[h, way, s, b], chip(y + 1 if way == 0 else y - 1, h)
        )

    def share_copy(h, j):
        ref = xbuf.at[chunk(j), pl.ds(h * rows, rows)]
        return remote(ref, ref, cs_sem.at[h, j + hop], cr_sem.at[h, j + hop], peer)

    def share(h, *chunks):
        for j in chunks:
            send(h, functools.partial(share_copy, h, j))

    def gemm(j, start=False):
        k = chunk(j)
        for h in range(2):

            @pl.when(jnp.logical_not(active[h]))
            def _():
                share_copy(h, j).wait_recv()

        lhs = xbuf[k]
        deep = pl.ds(pl.multiple_of(k * width, 128), width)
        for acc, w in ((acc_g, wg_v), (acc_u, wu_v)):
            term = jnp.dot(lhs, w[deep, :], preferred_element_type=F32)
            acc[...] = term if start else acc[...] + term

    carry(lambda h: x_send(h, 0))
    for i in range(1, len(direct)):
        loads[2 + i].wait()
        xs[i] = jnp.dot(picked, tok_v[i], preferred_element_type=F32).astype(BF16)
        carry(lambda h: x_send(h, i))

    def first_hop(h):
        for b in near_first:
            for t in others(b):
                n = (e + ne - t) % ne
                remote(
                    xs.at[0, slab(h, 0)],
                    xbuf.at[chunk(0), slab(h, t)],
                    xs_sem.at[h, 0, n],
                    xr_sem.at[h, 0, n],
                    across(t, h),
                ).wait_recv()
            for way in range(2):
                send(h, functools.partial(y_copy, h, way, 0, b))

    def next_hop(s, h):
        for b in near_first:
            for way in range(2):
                y_copy(h, way, s, b, True).wait_recv()
                if s + 1 < steps:
                    send(h, functools.partial(y_copy, h, way, s + 1, b))

    def x_rest(h, i):
        x_arrived(h, i)
        share(h, direct[i])

    def last_hop(h):
        next_hop(steps - 1, h)
        share(h, -steps, steps)

    carry(first_hop)

    @pl.when(jnp.logical_not(jnp.logical_or(double, lone)))
    def _():
        for h in range(2):

            @pl.when(active[h])
            def _():
                share_copy(h, 0).start()

    for s in range(steps - 1):
        carry(functools.partial(next_hop, s))

    @pl.when(double)
    def _():
        pl.semaphore_wait(ready, 1)
        share_copy(0, 0).start()
        share_copy(1, 0).start()

    for h in range(2):
        sent_of[h].append(functools.partial(share_copy, h, 0))
    carry(lambda h: share(h, *[j for k in range(1, steps) for j in (-k, k)]))
    ahead = len(pairs) - 3
    loads[ahead].wait()
    loads[ahead + 1].wait()
    gemm(0, True)
    carry(lambda h: x_rest(h, 1))
    for k in range(1, steps):
        gemm(-k)
        gemm(k)
    carry(lambda h: x_rest(h, 2))
    gemm(far)
    carry(last_hop)
    for i in range(3, len(direct)):
        carry(lambda h: x_rest(h, i))
    for j in (direct[2], -steps, steps, *direct[3:]):
        gemm(j)

    @pl.when(jnp.logical_or(beside, second_on))
    def _():
        pl.semaphore_wait(ready, 1)

    gate = acc_g[...]
    hid[...] = (gate / (1.0 + jnp.exp(-gate)) * acc_u[...]).astype(BF16)
    loads[ahead + 2].wait()

    low = lax.broadcasted_iota(jnp.int32, (rows, width), 1) < width // 2

    def down(j):
        i = j + hop
        cols = pl.ds(pl.multiple_of(chunk(j) * width, 128), width)
        part = jnp.dot(hid[...], wd_v[:, cols], preferred_element_type=F32)
        a, b = part[:rows], part[rows:]
        pk[i, 0] = jnp.where(low, a, pltpu.roll(b, width // 2, 1)).astype(BF16)
        pk[i, 1] = jnp.where(low, pltpu.roll(a, width // 2, 1), b).astype(BF16)
        go(remote(pk.at[i, 1 - c], cin.at[i], ds_sem.at[i], dr_sem.at[i], peer))

    def met(j):
        i = j + hop
        remote(pk.at[i, 1 - c], cin.at[i], ds_sem.at[i], dr_sem.at[i], peer).wait_recv()

    def own(j, b):
        i = j + hop
        at = pl.ds(part(b), sub)
        return pk[i, c, at, :].astype(F32) + cin[i, at, :].astype(F32)

    def r_copy(way, s, b):
        at = pl.ds(part(b), sub)
        return remote(
            rout.at[way, s, at],
            rin.at[way, s, at],
            rs_sem.at[way, s, b],
            rr_sem.at[way, s, b],
            two_on[way] if s == 0 else right if way == 0 else left,
        )

    def got(way, s, b):
        r_copy(way, s, b).wait_recv()
        return rin[way, s, pl.ds(part(b), sub), :].astype(F32)

    def pass_on(way, s, b):
        total = own(far - s if s == 0 or way == 0 else s - far, b)
        if s > 1:
            total = total + got(way, s - 1, b)
        if s == 2 and b // (parts // 2) == way:
            total = total + got(way, 0, b)
        rout[way, s, pl.ds(part(b), sub), :] = total.astype(BF16)
        go(r_copy(way, s, b))

    down(far)
    for j in range(far - 1, max(0, far - 3), -1):
        down(j)
        down(-j)
    early = (1, 0)
    met(far)
    for b in early:
        pass_on(0, 0, b)
        pass_on(1, 0, parts - 1 - b)
    met(far - 1)
    met(1 - far)
    for b in far_first_parts:
        pass_on(0, 1, b)
        pass_on(1, 1, b)
    for j in range(far - 3, 0, -1):
        down(j)
        down(-j)
    down(0)
    for s in range(2, far):
        met(far - s)
        met(s - far)
        for b in far_first_parts:
            pass_on(0, s, b)
            pass_on(1, s, b)
    met(0)

    own_back = pl.ds(at16(e * half), half)

    def back_copy(t):
        return remote(
            fin.at[pl.ds(at16(t * half), half)], rbuf.at[own_back], fs_sem.at[t], fr_sem.at[e], {"expert": t}
        )

    for b in far_first_parts:
        total = own(0, b) + got(0, far - 1, b) + got(1, far - 1, b)
        fin[pl.ds(part(b), sub), :] = total.astype(BF16)
        for t in others(b):
            back_copy(t).start()

    rbuf[own_back, :] = fin[own_back, :]
    weights = mix[...].T
    hi = weights.astype(BF16)
    lo = (weights - hi.astype(F32)).astype(BF16)
    for copy in sent:
        copy.wait_send()
    carry(lambda h: [make().wait_send() for make in sent_of[h]])
    for n in range(1, ne):
        t = (e + n) % ne
        at = pl.ds(at16(t * half), half)
        remote(fin.at[at], rbuf.at[at], fs_sem.at[t], fr_sem.at[t], {"expert": t}).wait()
    back = rbuf[...]

    def mixed(side):
        cols = slice(side * rows, side * rows + rows)
        return jnp.dot(hi[:, cols], back, preferred_element_type=F32) + jnp.dot(
            lo[:, cols], back, preferred_element_type=F32
        )

    total = mixed(0) + pltpu.roll(mixed(1), width // 2, 1)
    out[...] = total[:, : width // 2].astype(BF16)


def on_device(tokens, routes, route_weights, w_gate, w_up, w_down):
    ne = lax.axis_size("expert")
    ny = lax.axis_size("pipe") // 2
    toks, model = tokens.shape
    hidden = w_gate.shape[2]
    width = model // ny
    half = 16
    rows = ne * half
    far = ny // 2
    vmem = pl.BlockSpec(memory_space=pltpu.VMEM)
    hbm = pl.BlockSpec(memory_space=pl.ANY)
    dma = pltpu.SemaphoreType.DMA
    return pl.pallas_call(
        functools.partial(kernel, (ne, ny, half, width)),
        out_shape=jax.ShapeDtypeStruct((toks, width // 2), BF16),
        in_specs=[hbm] * 6,
        out_specs=vmem,
        scratch_shapes=[
            pltpu.VMEM((2, toks), jnp.int32),
            pltpu.VMEM((2, toks), F32),
            pltpu.VMEM((4, toks, width), BF16),
            pltpu.VMEM((4, 2 * rows, width), BF16),
            pltpu.VMEM((ny, 2 * rows, width), BF16),
            pltpu.VMEM((model, hidden), BF16),
            pltpu.VMEM((model, hidden), BF16),
            pltpu.VMEM((hidden, model), BF16),
            pltpu.VMEM((2 * rows, hidden), F32),
            pltpu.VMEM((2 * rows, hidden), F32),
            pltpu.VMEM((2 * rows, hidden), BF16),
            pltpu.VMEM((2 * rows, toks), F32),
            pltpu.VMEM((ny, 2, rows, width), BF16),
            pltpu.VMEM((ny, rows, width), BF16),
            pltpu.VMEM((2, far, rows, width), BF16),
            pltpu.VMEM((2, far, rows, width), BF16),
            pltpu.VMEM((rows, width), BF16),
            pltpu.VMEM((rows, width), BF16),
            dma((9,)),
            dma((2, 4, ne)),
            dma((2, 4, ne)),
            dma((2, 2, far - 2, 4)),
            dma((2, 2, far - 2, 4)),
            dma((2, ny)),
            dma((2, ny)),
            dma((ny,)),
            dma((ny,)),
            dma((2, far, 4)),
            dma((2, far, 4)),
            dma((ne,)),
            dma((ne,)),
            pltpu.SemaphoreType.REGULAR,
        ],
        compiler_params=pltpu.CompilerParams(
            collective_id=0, has_side_effects=True, vmem_limit_bytes=54784 * 1024
        ),
    )(tokens, routes.T, route_weights.T, w_gate, w_up, w_down)


def solution(mesh):
    return jax.shard_map(
        on_device,
        mesh=mesh,
        in_specs=(
            P(("dp", "expert"), None),
            P(("dp", "expert"), None),
            P(("dp", "expert"), None),
            P("expert", None, "pipe"),
            P("expert", None, "pipe"),
            P("expert", "pipe", None),
        ),
        out_specs=P(("dp", "expert"), "pipe"),
        check_vma=False,
    )
```

```python
import functools

import jax
import jax.numpy as jnp
from jax import lax
from jax.experimental import pallas as pl
from jax.experimental.pallas import tpu as pltpu
from jax.sharding import PartitionSpec as P

MESH = pl.DeviceIdType.MESH
F32 = jnp.float32
BF16 = jnp.bfloat16


def kernel(
    dims,
    tokens,
    routes,
    route_w,
    wg,
    wu,
    wd,
    out,
    route_v,
    weight_v,
    tok_v,
    xs,
    xbuf,
    wg_v,
    wu_v,
    wd_v,
    acc_g,
    acc_u,
    hid,
    mix,
    pk,
    cin,
    rin,
    rout,
    fin,
    rbuf,
    load_sem,
    xs_sem,
    xr_sem,
    ys_sem,
    yr_sem,
    cs_sem,
    cr_sem,
    ds_sem,
    dr_sem,
    rs_sem,
    rr_sem,
    fs_sem,
    fr_sem,
    ready,
):
    ne, ny, half, width = dims
    rows = ne * half
    parts = 4
    sub = rows // parts
    per = ne // parts
    pipe = lax.axis_index("pipe")
    e = lax.axis_index("expert")
    y = pipe // 2
    c = pipe % 2
    d = lax.axis_index("dp")
    far = ny // 2
    hop = far - 1
    steps = far - 2

    def zero(v, n):
        return 1 - (v + n - 1) // n

    def carrier(at_y, at_e, h):
        if h == 1:
            return 1
        return zero(d, lax.axis_size("dp")) * zero(at_y, ny) * zero(at_e, ne)

    def chip(at_y, h):
        at_y = (at_y + ny) % ny
        return {"pipe": 2 * at_y + carrier(at_y, e, h)}

    def across(t, h):
        return {"pipe": 2 * y + carrier(y, t, h), "expert": t}

    right = {"pipe": (y + 1) % ny * 2 + c}
    left = {"pipe": (y + ny - 1) % ny * 2 + c}
    peer = {"pipe": 2 * y + 1 - c}
    two_on = [{"pipe": (y + 2) % ny * 2 + c}, {"pipe": (y + ny - 2) % ny * 2 + c}]
    front = d == 0
    lone = jnp.logical_and(front, jnp.logical_and(pipe == 0, e == 0))
    double = jnp.logical_and(front, jnp.logical_and(pipe == 1, e == 0))
    in_row = jnp.logical_and(y == 0, e != 0)
    in_column = jnp.logical_and(e == 0, jnp.logical_or(y == 1, y == ny - 1))
    in_second = jnp.logical_and(e == 0, jnp.logical_or(y == 2, y == ny - 2))
    second_on = jnp.logical_and(jnp.logical_and(front, c == 0), in_second)
    beside = jnp.logical_and(jnp.logical_and(front, c == 0), jnp.logical_or(in_row, in_column))
    active = [carrier(y, e, h) == c for h in range(2)]

    def chunk(j):
        return (y + j + ny) % ny

    base = e // per
    near_first, far_first_parts = (0, 1, 3, 2), (2, 1, 3, 0)

    def part(k):
        return pl.multiple_of((base + k) % parts * sub, sub)

    def others(k):
        if k:
            return [(base + k) % parts * per + m for m in range(per)]
        return [base * per + (e + m) % per for m in range(1, per)]

    def at16(x):
        return pl.multiple_of(x, 16)

    def remote(src, dst, send, recv, device):
        return pltpu.make_async_remote_copy(
            src_ref=src, dst_ref=dst, send_sem=send, recv_sem=recv, device_id=device, device_id_type=MESH
        )

    sent = []
    sent_of = [[], []]

    def go(copy):
        copy.start()
        sent.append(copy)

    def send(h, make):
        make().start()
        sent_of[h].append(make)

    def carry(work):
        for h in range(2):

            @pl.when(active[h])
            def _():
                work(h)

    pairs = [(routes, route_v), (route_w, weight_v)]
    direct = [0, far] + [j for k in range(steps + 1, far) for j in (-k, k)]
    for i, j in enumerate(direct):
        cols = pl.ds(pl.multiple_of(chunk(j) * width, 128), width)
        pairs.append((tokens.at[:, cols], tok_v.at[i]))
    pairs += [(wg.at[0], wg_v), (wu.at[0], wu_v), (wd.at[0], wd_v)]
    loads = [pltpu.make_async_copy(src, dst, load_sem.at[i]) for i, (src, dst) in enumerate(pairs)]
    for copy in loads:
        copy.start()

    barrier = pltpu.get_barrier_semaphore()

    def greet(semaphore, device):
        pl.semaphore_signal(semaphore, inc=1, device_id=device, device_id_type=MESH)

    neighbours = [{"expert": (e + j) % ne} for j in range(1, ne)] + [right, left, peer, *two_on]

    @pl.when(jnp.logical_not(lone))
    def _():
        for device in neighbours:
            greet(barrier, device)

    @pl.when(double)
    def _():
        for device in [{"pipe": 0, "expert": t} for t in range(1, ne)] + [{"pipe": 2}, {"pipe": 2 * ny - 2}]:
            greet(barrier, device)

    @pl.when(beside)
    def _():
        greet(barrier, {"pipe": 1, "expert": 0})

    toks = tok_v.shape[1]
    row = lax.broadcasted_iota(jnp.int32, (2 * rows, toks), 0)
    hbits, rbits = half.bit_length() - 1, rows.bit_length() - 1
    expert_of = (row >> hbits) & (ne - 1)
    slot_of = ((row >> rbits) << hbits) + (row & (half - 1))
    loads[0].wait()
    loads[1].wait()
    first = route_v[0:1, :] == expert_of
    second = route_v[1:2, :] == expert_of
    named = jnp.logical_or(first, second)
    before = (
        lax.broadcasted_iota(jnp.int32, (toks, toks), 0) < lax.broadcasted_iota(jnp.int32, (toks, toks), 1)
    ).astype(F32)
    rank = jnp.dot(named.astype(F32).astype(BF16), before.astype(BF16), preferred_element_type=F32)
    taken = jnp.logical_and(named, rank == slot_of.astype(F32))
    mix[...] = jnp.where(taken, jnp.where(first, weight_v[0:1, :], weight_v[1:2, :]), 0.0)
    picked = taken.astype(F32)
    picked = picked.astype(BF16)
    loads[2].wait()
    xs[0] = jnp.dot(picked, tok_v[0], preferred_element_type=F32).astype(BF16)

    @pl.when(jnp.logical_not(jnp.logical_or(double, second_on)))
    def _():
        pl.semaphore_wait(barrier, len(neighbours))

    @pl.when(second_on)
    def _():
        pl.semaphore_wait(barrier, len(neighbours) - 1)

    @pl.when(double)
    def _():
        pl.semaphore_wait(barrier, len(neighbours) - 1 + ne - 1 + 2)

    @pl.when(lone)
    def _():
        for device in neighbours:
            greet(ready, device)

    far_first = sorted(range(1, ne), key=lambda n: -min(n, ne - n))

    def slab(core, t):
        return pl.ds(at16(core * rows + t * half), half)

    def x_copy(h, i, n):
        t = (e + n) % ne
        return remote(
            xs.at[i, slab(h, t)],
            xbuf.at[chunk(direct[i]), slab(h, e)],
            xs_sem.at[h, i, n],
            xr_sem.at[h, i, n],
            across(t, h),
        )

    def x_send(h, i):
        for n in far_first:
            send(h, functools.partial(x_copy, h, i, n))
        xbuf[chunk(direct[i]), slab(h, e), :] = xs[i, slab(h, e), :]

    def x_arrived(h, i):
        for n in reversed(far_first):
            t = (e + ne - n) % ne
            remote(
                xs.at[i, slab(h, 0)],
                xbuf.at[chunk(direct[i]), slab(h, t)],
                xs_sem.at[h, i, n],
                xr_sem.at[h, i, n],
                across(t, h),
            ).wait_recv()

    def y_copy(h, way, s, b, arriving=False):
        j = s + 1 if arriving else s
        ref = xbuf.at[chunk(-j if way == 0 else j), pl.ds(pl.multiple_of(h * rows + part(b), sub), sub)]
        return remote(
            ref, ref, ys_sem.at[h, way, s, b], yr_sem.at[h, way, s, b], chip(y + 1 if way == 0 else y - 1, h)
        )

    def share_copy(h, j):
        ref = xbuf.at[chunk(j), pl.ds(h * rows, rows)]
        return remote(ref, ref, cs_sem.at[h, j + hop], cr_sem.at[h, j + hop], peer)

    def share(h, *chunks):
        for j in chunks:
            send(h, functools.partial(share_copy, h, j))

    def gemm(j, start=False):
        k = chunk(j)
        for h in range(2):

            @pl.when(jnp.logical_not(active[h]))
            def _():
                share_copy(h, j).wait_recv()

        lhs = xbuf[k]
        deep = pl.ds(pl.multiple_of(k * width, 128), width)
        for acc, w in ((acc_g, wg_v), (acc_u, wu_v)):
            term = jnp.dot(lhs, w[deep, :], preferred_element_type=F32)
            acc[...] = term if start else acc[...] + term

    carry(lambda h: x_send(h, 0))
    for i in range(1, len(direct)):
        loads[2 + i].wait()
        xs[i] = jnp.dot(picked, tok_v[i], preferred_element_type=F32).astype(BF16)
        carry(lambda h: x_send(h, i))

    def first_hop(h):
        for b in near_first:
            for t in others(b):
                n = (e + ne - t) % ne
                remote(
                    xs.at[0, slab(h, 0)],
                    xbuf.at[chunk(0), slab(h, t)],
                    xs_sem.at[h, 0, n],
                    xr_sem.at[h, 0, n],
                    across(t, h),
                ).wait_recv()
            for way in range(2):
                send(h, functools.partial(y_copy, h, way, 0, b))

    def next_hop(s, h):
        for b in near_first:
            for way in range(2):
                y_copy(h, way, s, b, True).wait_recv()
                if s + 1 < steps:
                    send(h, functools.partial(y_copy, h, way, s + 1, b))

    def x_rest(h, i):
        x_arrived(h, i)
        share(h, direct[i])

    def last_hop(h):
        next_hop(steps - 1, h)
        share(h, -steps, steps)

    carry(first_hop)

    @pl.when(jnp.logical_not(jnp.logical_or(double, lone)))
    def _():
        for h in range(2):

            @pl.when(active[h])
            def _():
                share_copy(h, 0).start()

    for s in range(steps - 1):
        carry(functools.partial(next_hop, s))

    @pl.when(double)
    def _():
        pl.semaphore_wait(ready, 1)
        share_copy(0, 0).start()
        share_copy(1, 0).start()

    for h in range(2):
        sent_of[h].append(functools.partial(share_copy, h, 0))
    carry(lambda h: share(h, *[j for k in range(1, steps) for j in (-k, k)]))
    ahead = len(pairs) - 3
    loads[ahead].wait()
    loads[ahead + 1].wait()
    gemm(0, True)
    carry(lambda h: x_rest(h, 1))
    for k in range(1, steps):
        gemm(-k)
        gemm(k)
    carry(lambda h: x_rest(h, 2))
    gemm(far)
    carry(last_hop)
    for i in range(3, len(direct)):
        carry(lambda h: x_rest(h, i))
    for j in (direct[2], -steps, steps, *direct[3:]):
        gemm(j)

    @pl.when(jnp.logical_or(beside, second_on))
    def _():
        pl.semaphore_wait(ready, 1)

    gate = acc_g[...]
    hid[...] = (gate / (1.0 + jnp.exp(-gate)) * acc_u[...]).astype(BF16)
    loads[ahead + 2].wait()

    low = lax.broadcasted_iota(jnp.int32, (rows, width), 1) < width // 2

    def down(j):
        i = j + hop
        cols = pl.ds(pl.multiple_of(chunk(j) * width, 128), width)
        part = jnp.dot(hid[...], wd_v[:, cols], preferred_element_type=F32)
        a, b = part[:rows], part[rows:]
        pk[i, 0] = jnp.where(low, a, pltpu.roll(b, width // 2, 1)).astype(BF16)
        pk[i, 1] = jnp.where(low, pltpu.roll(a, width // 2, 1), b).astype(BF16)
        go(remote(pk.at[i, 1 - c], cin.at[i], ds_sem.at[i], dr_sem.at[i], peer))

    def met(j):
        i = j + hop
        remote(pk.at[i, 1 - c], cin.at[i], ds_sem.at[i], dr_sem.at[i], peer).wait_recv()

    def own(j, b):
        i = j + hop
        at = pl.ds(part(b), sub)
        return pk[i, c, at, :].astype(F32) + cin[i, at, :].astype(F32)

    def r_copy(way, s, b):
        at = pl.ds(part(b), sub)
        return remote(
            rout.at[way, s, at],
            rin.at[way, s, at],
            rs_sem.at[way, s, b],
            rr_sem.at[way, s, b],
            two_on[way] if s == 0 else right if way == 0 else left,
        )

    def got(way, s, b):
        r_copy(way, s, b).wait_recv()
        return rin[way, s, pl.ds(part(b), sub), :].astype(F32)

    def pass_on(way, s, b):
        total = own(far - s if s == 0 or way == 0 else s - far, b)
        if s > 1:
            total = total + got(way, s - 1, b)
        if s == 2 and b // (parts // 2) == way:
            total = total + got(way, 0, b)
        rout[way, s, pl.ds(part(b), sub), :] = total.astype(BF16)
        go(r_copy(way, s, b))

    down(far)
    for j in (far - 1,):
        down(j)
        down(-j)
    early = (1, 0)
    met(far)
    for b in early:
        pass_on(0, 0, b)
        pass_on(1, 0, parts - 1 - b)
    met(far - 1)
    met(1 - far)
    for b in far_first_parts:
        pass_on(0, 1, b)
        pass_on(1, 1, b)
    for j in range(far - 2, 0, -1):
        down(j)
        down(-j)
    down(0)
    for s in range(2, far):
        met(far - s)
        met(s - far)
        for b in far_first_parts:
            pass_on(0, s, b)
            pass_on(1, s, b)
    met(0)

    own_back = pl.ds(at16(e * half), half)

    def back_copy(t):
        return remote(
            fin.at[pl.ds(at16(t * half), half)], rbuf.at[own_back], fs_sem.at[t], fr_sem.at[e], {"expert": t}
        )

    for b in far_first_parts:
        total = own(0, b) + got(0, far - 1, b) + got(1, far - 1, b)
        fin[pl.ds(part(b), sub), :] = total.astype(BF16)
        for t in others(b):
            back_copy(t).start()

    rbuf[own_back, :] = fin[own_back, :]
    weights = mix[...].T
    hi = weights.astype(BF16)
    lo = (weights - hi.astype(F32)).astype(BF16)
    for copy in sent:
        copy.wait_send()
    carry(lambda h: [make().wait_send() for make in sent_of[h]])
    for n in range(1, ne):
        t = (e + n) % ne
        at = pl.ds(at16(t * half), half)
        remote(fin.at[at], rbuf.at[at], fs_sem.at[t], fr_sem.at[t], {"expert": t}).wait()
    back = rbuf[...]

    def mixed(side):
        cols = slice(side * rows, side * rows + rows)
        return jnp.dot(hi[:, cols], back, preferred_element_type=F32) + jnp.dot(
            lo[:, cols], back, preferred_element_type=F32
        )

    total = mixed(0) + pltpu.roll(mixed(1), width // 2, 1)
    out[...] = total[:, : width // 2].astype(BF16)


def on_device(tokens, routes, route_weights, w_gate, w_up, w_down):
    ne = lax.axis_size("expert")
    ny = lax.axis_size("pipe") // 2
    toks, model = tokens.shape
    hidden = w_gate.shape[2]
    width = model // ny
    half = 16
    rows = ne * half
    far = ny // 2
    vmem = pl.BlockSpec(memory_space=pltpu.VMEM)
    hbm = pl.BlockSpec(memory_space=pl.ANY)
    dma = pltpu.SemaphoreType.DMA
    return pl.pallas_call(
        functools.partial(kernel, (ne, ny, half, width)),
        out_shape=jax.ShapeDtypeStruct((toks, width // 2), BF16),
        in_specs=[hbm] * 6,
        out_specs=vmem,
        scratch_shapes=[
            pltpu.VMEM((2, toks), jnp.int32),
            pltpu.VMEM((2, toks), F32),
            pltpu.VMEM((4, toks, width), BF16),
            pltpu.VMEM((4, 2 * rows, width), BF16),
            pltpu.VMEM((ny, 2 * rows, width), BF16),
            pltpu.VMEM((model, hidden), BF16),
            pltpu.VMEM((model, hidden), BF16),
            pltpu.VMEM((hidden, model), BF16),
            pltpu.VMEM((2 * rows, hidden), F32),
            pltpu.VMEM((2 * rows, hidden), F32),
            pltpu.VMEM((2 * rows, hidden), BF16),
            pltpu.VMEM((2 * rows, toks), F32),
            pltpu.VMEM((ny, 2, rows, width), BF16),
            pltpu.VMEM((ny, rows, width), BF16),
            pltpu.VMEM((2, far, rows, width), BF16),
            pltpu.VMEM((2, far, rows, width), BF16),
            pltpu.VMEM((rows, width), BF16),
            pltpu.VMEM((rows, width), BF16),
            dma((9,)),
            dma((2, 4, ne)),
            dma((2, 4, ne)),
            dma((2, 2, far - 2, 4)),
            dma((2, 2, far - 2, 4)),
            dma((2, ny)),
            dma((2, ny)),
            dma((ny,)),
            dma((ny,)),
            dma((2, far, 4)),
            dma((2, far, 4)),
            dma((ne,)),
            dma((ne,)),
            pltpu.SemaphoreType.REGULAR,
        ],
        compiler_params=pltpu.CompilerParams(
            collective_id=0, has_side_effects=True, vmem_limit_bytes=54784 * 1024
        ),
    )(tokens, routes.T, route_weights.T, w_gate, w_up, w_down)


def solution(mesh):
    return jax.shard_map(
        on_device,
        mesh=mesh,
        in_specs=(
            P(("dp", "expert"), None),
            P(("dp", "expert"), None),
            P(("dp", "expert"), None),
            P("expert", None, "pipe"),
            P("expert", None, "pipe"),
            P("expert", "pipe", None),
        ),
        out_specs=P(("dp", "expert"), "pipe"),
        check_vma=False,
    )
```
